128 devices in a mesh: segment: 4 (over x), seq: 32 (over z, y, core).
Axes of the slice: x: 4, y: 4, z: 4, core: 2. Of those that a mesh axis runs over, the one named last changes fastest.
Arguments:
- hidden: bfloat16 [4, 32768, 8192], P('segment', 'seq'), may hold values from -6 to 6
- span_lengths: int32 [4, 256], replicated, may hold values from 1 to 512, 32768 in all within a row
- section_of: int32 [4, 256], replicated, may hold values from 0 to 127
- section_live: int32 [128], P('seq'), may hold values 0 or 1
- w_in: bfloat16 [8192, 2048], P('seq'), may hold values from -0.5 to 0.5
- norm_gain: float32 [2048], replicated, may hold values from 0.5 to 1.5
- w_query: bfloat16 [2048, 2048], P(None, 'segment'), may hold values from -0.125 to 0.125
- w_key: bfloat16 [2048, 2048], P(None, 'segment'), may hold values from -0.125 to 0.125
- w_value: bfloat16 [2048, 2048], P(None, 'segment'), may hold values from -0.125 to 0.125
- w_out: bfloat16 [2048, 2048], P('segment'), may hold values from -0.125 to 0.125
Outputs:
- section_out: bfloat16 [128, 2048], P('seq')
The draws below stay inside these ranges and needn't reach their ends.
All inputs are finite; a program needn't handle non-finite values. No bound on the sum of `section_live` on one device may be relied on, other than what follows from the above.
Results may differ from the reference program's by a relative error of at most 0.007.
Values may be sent and summed in bfloat16 or wider, within the bound.
No kernel may reach another device: no remote copies, remote signals or barrier semaphores. Data moves between devices by JAX's collectives and lax.ppermute only.
A program may use at most 128 MiB of HBM per device.

```python
import math
import jax
import jax.numpy as jnp
import numpy as np
from jax import lax

D = 8192
DS = 2048
HEADS = 16
HEAD_DIM = 128
SPAN_MAX = 512
DOCS = 4
L = 32768
NCH = 256
NSEC = 128


def with_ends(entries, own_key, smallest, largest):
    longest = entries.shape.index(max(entries.shape))
    spots = []
    for shift in (0, 1):
        where = [jax.random.randint(jax.random.fold_in(own_key, axis), (), 0, length) for axis, length in enumerate(entries.shape)]
        where[longest] = (where[longest] + shift) % entries.shape[longest]
        spots.append(tuple(where))
    return entries.at[spots[0]].set(smallest).at[spots[1]].set(largest)


def levels(rng, extent, pieces, low, top_value):
    gain = 1.0
    for position, blocks in pieces:
        steps = jax.random.uniform(jax.random.fold_in(jax.random.fold_in(rng, 6), position), (blocks,), jnp.float32, low / len(pieces), top_value / len(pieces))
        gain = gain * jnp.repeat(jnp.exp(steps), extent[position] // blocks).reshape((-1,) + (1,) * (len(extent) - 1 - position))
    return gain


def rank_table(amount, slope):
    weights = [(1 << 20) // math.isqrt(rank ** slope) + 1 for rank in range(1, amount + 1)]
    spread = 1 + sum(weights) // (1 << 30)
    return np.cumsum(np.array([max(1, weight // spread) for weight in weights]))


def skewed_ids(stream_key, shape, amount, skew):
    grid = rank_table(amount, skew)
    ticket = jax.random.randint(jax.random.fold_in(stream_key, 1), shape, 0, int(grid[amount - 1]))
    rank = jnp.searchsorted(jnp.asarray(grid, jnp.int32), ticket, side="right")
    return jax.random.permutation(jax.random.fold_in(stream_key, 2), amount)[rank].astype(jnp.int32)


def profile(count, total, most, slope):
    weights = [(1 << 20) // math.isqrt(standing ** slope) + 1 for standing in range(2, count + 1)]
    surplus, given = total - most - (count - 1), [1] * (count - 1)
    while surplus > 0:
        free = [i for i in range(count - 1) if given[i] < most]
        pool, remaining = sum([weights[i] for i in free]), surplus
        for i in free:
            extra = min(most - given[i], max(1, remaining * weights[i] // pool), surplus)
            given[i] = given[i] + extra
            surplus = surplus - extra
    return np.array([most] + given)


def ragged_sizes(rng, number_of, total, most, lean):
    if number_of == 2:
        one = jax.random.randint(rng, (), max(1, total - most), min(most, total - 1) + 1)
        return jnp.stack([one, total - one])
    lengths = jnp.asarray(profile(number_of, total, most, lean), jnp.int32)
    pairs = (number_of - 1) // 2
    donor, receiver = lengths[1:1 + 2 * pairs:2], lengths[2:2 + 2 * pairs:2]
    room = jnp.minimum(donor - 1, most - receiver)
    passed = jax.random.randint(jax.random.fold_in(rng, 1), (pairs,), 0, 1 << 20) % (room + 1)
    lengths = lengths.at[1:1 + 2 * pairs:2].set(donor - passed).at[2:2 + 2 * pairs:2].set(receiver + passed)
    return lengths[jax.random.permutation(jax.random.fold_in(rng, 2), number_of)]


def centred(rng, shape, deviation, most, shards=(), held_as=jnp.bfloat16):
    result = deviation * jax.random.normal(rng, shape, jnp.float32)
    if shards:
        result = result * levels(rng, shape, shards, -0.22, 0.18)
    return jnp.clip(result, -most, most).astype(held_as)


def setup_inputs(seed: int = 0) -> dict:
    keys = jax.random.split(jax.random.key(seed), 11)
    hidden = centred(keys[0], (DOCS, L, D), 1.0, 6.0, ((0, 4), (1, 32)))
    span_lengths = jax.vmap(lambda own: ragged_sizes(own, NCH, L, SPAN_MAX, 2))(jax.random.split(keys[1], DOCS)).reshape((DOCS, NCH)).astype(jnp.int32)
    section_of = with_ends(skewed_ids(keys[2], (DOCS, NCH), NSEC, 2), jax.random.fold_in(keys[2], 3), 0, NSEC - 1).astype(jnp.int32)
    section_live = with_ends((jax.random.randint(keys[3], (NSEC,), 0, 4) < 3).astype(jnp.int32), jax.random.fold_in(keys[3], 1), 0, 1)
    w_in = centred(keys[4], (D, DS), (D // 64) ** -0.5, 0.5, ((0, 32),))
    norm_gain = jnp.clip(1.0 + 0.1 * jax.random.normal(keys[5], (DS,), jnp.float32), 0.5, 1.5)
    w_query = centred(keys[6], (DS, DS), DS ** -0.5, 0.125, ((1, 4),))
    w_key = centred(keys[7], (DS, DS), DS ** -0.5, 0.125, ((1, 4),))
    w_value = centred(keys[8], (DS, DS), DS ** -0.5, 0.125, ((1, 4),))
    w_out = centred(keys[9], (DS, DS), DS ** -0.5, 0.125, ((0, 4),))
    return {"hidden": hidden, "span_lengths": span_lengths, "section_of": section_of, "section_live": section_live, "w_in": w_in, "norm_gain": norm_gain, "w_query": w_query, "w_key": w_key, "w_value": w_value, "w_out": w_out}


def reference(hidden, span_lengths, section_of, section_live, w_in, norm_gain, w_query, w_key, w_value, w_out):
    span_ends = jnp.cumsum(span_lengths, axis=1).astype(jnp.int32)
    span_starts = (span_ends - span_lengths).astype(jnp.int32)
    positions = jnp.arange(L, dtype=jnp.int32)

    def pool_document(packed):
        tokens, starts, stops = packed
        member = ((positions[None, :] >= starts[:, None]) & (positions[None, :] < stops[:, None])).astype(jnp.bfloat16)
        return jnp.dot(member, tokens, preferred_element_type=jnp.float32)
    span_sums = lax.map(pool_document, (hidden, span_starts, span_ends))
    span_means = span_sums / span_lengths[:, :, None].astype(jnp.float32)
    flat_sections = section_of.reshape(-1)
    onehot = (jnp.arange(NSEC, dtype=jnp.int32)[:, None] == flat_sections[None, :]).astype(jnp.float32)
    section_sums = jnp.dot(onehot, span_means.reshape(-1, D), precision=lax.Precision.HIGHEST)
    section_count = lax.optimization_barrier(jnp.sum(onehot, axis=1))
    section_pooled = (section_sums / jnp.maximum(section_count, 1.0)[:, None]).astype(jnp.bfloat16)
    section_in = jnp.dot(section_pooled, w_in, preferred_element_type=jnp.float32)
    scale = lax.rsqrt(lax.optimization_barrier(jnp.mean(section_in * section_in, axis=1, keepdims=True)) + 1e-05)
    normed = (section_in * scale * norm_gain[None, :]).astype(jnp.bfloat16)
    queries = jnp.dot(normed, w_query, preferred_element_type=jnp.float32).astype(jnp.bfloat16)
    keys_all = jnp.dot(normed, w_key, preferred_element_type=jnp.float32).astype(jnp.bfloat16)
    values_all = jnp.dot(normed, w_value, preferred_element_type=jnp.float32).astype(jnp.bfloat16)
    query_heads = queries.reshape(NSEC, HEADS, HEAD_DIM).astype(jnp.float32)
    key_heads = keys_all.reshape(NSEC, HEADS, HEAD_DIM).astype(jnp.float32)
    value_heads = values_all.reshape(NSEC, HEADS, HEAD_DIM).astype(jnp.float32)
    scores = jnp.einsum('qhd,khd->hqk', query_heads, key_heads) / jnp.sqrt(jnp.float32(HEAD_DIM))
    section_ids = jnp.arange(NSEC, dtype=jnp.int32)
    allowed = (section_live[None, :] > 0) | (section_ids[None, :] == section_ids[:, None])
    scores = jnp.where(allowed[None, :, :], scores, jnp.float32(-1e+30))
    probs = jax.nn.softmax(scores, axis=-1).astype(jnp.bfloat16)
    attended = jnp.einsum('hqk,khd->qhd', probs.astype(jnp.float32), value_heads).astype(jnp.bfloat16)
    attended = attended.reshape(NSEC, DS)
    mixed = section_in + jnp.dot(attended, w_out, preferred_element_type=jnp.float32)
    return mixed.astype(jnp.bfloat16)
```

```python
import functools

import jax
import jax.numpy as jnp
from jax import lax
from jax.experimental import pallas as pl
from jax.experimental.pallas import tpu as pltpu
from jax.sharding import PartitionSpec as P

HEAD_DIM = 128
SLOTS = 32
F32 = jnp.float32
BF16 = jnp.bfloat16
I32 = jnp.int32


def iota(shape, dim):
    return lax.broadcasted_iota(I32, shape, dim)


def column_of(row):
    count = row.shape[1]
    same = iota((count, count), 0) == iota((count, count), 1)
    return jnp.sum(jnp.where(same, row, 0), axis=1, keepdims=True)


def pool_kernel(
    slots, peers, chunks, hidden, lens, secs, rows, place, most, buf, sems
):
    docs, spans = lens.shape
    toks, width = buf.shape
    step = width // chunks
    copies = [
        pltpu.make_async_copy(
            hidden.at[0, :, pl.ds(j * step, step)], buf.at[:, pl.ds(j * step, step)], sems.at[j]
        )
        for j in range(chunks)
    ]
    for copy in copies:
        copy.start()
    doc = lax.axis_index("segment")
    here = lax.axis_index("seq")
    tok0 = here * toks

    def pick(ref):
        return jnp.sum(jnp.where(iota((docs, spans), 0) == doc, ref[...], 0), axis=0, keepdims=True)

    len_row = pick(lens)
    sec_row = pick(secs)
    len_col = column_of(len_row)
    sec_col = column_of(sec_row)
    upto = iota((spans, spans), 0) <= iota((spans, spans), 1)
    end_row = jnp.sum(jnp.where(upto, len_col, 0), axis=0, keepdims=True)
    end_col = column_of(end_row)
    first = jnp.sum((end_row <= tok0).astype(I32), axis=1, keepdims=True)
    mine = iota((slots, spans), 1) == iota((slots, spans), 0) + first

    def slot(row):
        return jnp.sum(jnp.where(mine, row, 0), axis=1, keepdims=True)

    stop = slot(end_row)
    length = slot(len_row)
    section = slot(sec_row)
    count = jnp.zeros((slots, 1), F32)
    for d in range(docs):
        count = count + jnp.sum((secs[d : d + 1, :] == section).astype(F32), axis=1, keepdims=True)
    at = tok0 + iota((slots, toks), 1)
    member = ((at >= stop - length) & (at < stop)).astype(BF16)
    per_len = 1.0 / jnp.maximum(length, 1).astype(F32)
    per_count = 1.0 / jnp.maximum(count, 1.0)

    peer_width = width // peers
    for j in range(chunks):
        copies[j].wait()
        part = jnp.dot(member, buf[:, j * step : (j + 1) * step], preferred_element_type=F32)
        part = (part * per_len * per_count).astype(BF16)
        for i in range(step // peer_width):
            rows[j * (step // peer_width) + i] = part[:, i * peer_width : (i + 1) * peer_width]

    total = place.shape[1]
    lanes = 1024

    @pl.loop(0, total // lanes)
    def _(block):
        r = block * lanes + iota((1, lanes), 1)
        owner = r // slots
        begin = jnp.sum((end_col <= owner * toks).astype(I32), axis=0, keepdims=True)
        span = begin + (r - owner * slots)
        sec = jnp.sum(jnp.where(iota((spans, 1), 0) == span, sec_col, 0), axis=0, keepdims=True)
        hit = (iota((place.shape[0], 1), 0) == sec).astype(F32).astype(BF16)
        place[:, pl.ds(pl.multiple_of(block * lanes, lanes), lanes)] = hit

    worst = jnp.zeros((1, 1), I32)
    low = iota((1, 128), 1) * toks
    for d in range(docs):
        lcol = column_of(lens[d : d + 1, :])
        erow = jnp.sum(jnp.where(upto, lcol, 0), axis=0, keepdims=True)
        ecol = column_of(erow)
        held = jnp.sum(
            ((ecol > low) & (ecol - lcol < low + toks)).astype(I32), axis=0, keepdims=True
        )
        worst = jnp.maximum(worst, jnp.max(held, axis=1, keepdims=True))
    most[0, 0] = jnp.max(worst)


def pool(hidden, span_lengths, section_of, slots, peers, sections):
    toks, width = hidden.shape[1:]
    chunks = 16
    return pl.pallas_call(
        functools.partial(pool_kernel, slots, peers, chunks),
        out_shape=(
            jax.ShapeDtypeStruct((peers, slots, width // peers), BF16),
            jax.ShapeDtypeStruct((sections, peers * slots), BF16),
            jax.ShapeDtypeStruct((1, 1), I32),
        ),
        in_specs=[
            pl.BlockSpec(memory_space=pl.ANY),
            pl.BlockSpec(memory_space=pltpu.VMEM),
            pl.BlockSpec(memory_space=pltpu.VMEM),
        ],
        out_specs=(
            pl.BlockSpec(memory_space=pltpu.VMEM),
            pl.BlockSpec(memory_space=pltpu.VMEM),
            pl.BlockSpec(memory_space=pltpu.SMEM),
        ),
        scratch_shapes=[
            pltpu.VMEM((toks, width), BF16),
            pltpu.SemaphoreType.DMA((chunks,)),
        ],
        compiler_params=pltpu.CompilerParams(vmem_limit_bytes=48 * 1024 * 1024),
        name="pool",
    )(hidden, span_lengths, section_of)


def regroup(rows, place):
    got = lax.all_to_all(rows, "seq", 0, 0, tiled=True)
    got = got.reshape(-1, got.shape[-1])
    return jnp.dot(place, got, preferred_element_type=F32).astype(BF16)


def spread(block, axis):
    size = lax.axis_size(axis)
    return lax.all_to_all(jnp.broadcast_to(block[None], (size,) + block.shape), axis, 0, 0, tiled=True)


def shards(
    hidden, span_lengths, section_of, section_live, w_in, norm_gain, w_query, w_key, w_value, w_out
):
    peers = lax.axis_size("seq")
    seq_index = lax.axis_index("seq")
    sections_here = section_live.shape[0]
    sections = sections_here * peers
    spans = span_lengths.shape[1]
    rows, place, most = pool(hidden, span_lengths, section_of, SLOTS, peers, sections)

    def few(_):
        return regroup(rows, place)

    def many(_):
        all_rows, all_place, _ = pool(hidden, span_lengths, section_of, spans, peers, sections)
        return regroup(all_rows, all_place)

    pooled = lax.cond(most[0, 0] <= SLOTS, few, many, 0)
    projected = jnp.dot(pooled, w_in, preferred_element_type=F32).astype(BF16)
    projected = lax.all_to_all(
        projected.reshape(peers, sections_here, -1), "seq", 0, 0, tiled=True
    )
    doc_in = jnp.sum(projected.astype(F32), axis=0)
    section_in = jnp.sum(spread(doc_in, "segment"), axis=0)
    scale = lax.rsqrt(jnp.mean(section_in * section_in, axis=1, keepdims=True) + 1e-05)
    normed = (section_in * scale * norm_gain[None, :]).astype(BF16)
    keys_here = jnp.dot(normed, w_key, preferred_element_type=F32).astype(BF16)
    values_here = jnp.dot(normed, w_value, preferred_element_type=F32).astype(BF16)
    cols = keys_here.shape[1]
    live_here = jnp.broadcast_to(section_live[:, None], (sections_here, 128)).astype(BF16)
    packed = spread(jnp.concatenate([keys_here, values_here, live_here], axis=1), "seq")
    queries = jnp.dot(normed, w_query, preferred_element_type=F32).astype(BF16)
    packed = packed.reshape(sections, -1)
    keys_all, values_all, live_all = (
        packed[:, :cols],
        packed[:, cols : 2 * cols],
        packed[:, 2 * cols],
    )
    heads = cols // HEAD_DIM
    query_heads = queries.reshape(sections_here, heads, HEAD_DIM)
    key_heads = keys_all.reshape(sections, heads, HEAD_DIM)
    value_heads = values_all.reshape(sections, heads, HEAD_DIM)
    scores = jnp.einsum("qhd,khd->hqk", query_heads, key_heads, preferred_element_type=F32)
    scores = scores / jnp.sqrt(F32(HEAD_DIM))
    own = seq_index * sections_here + jnp.arange(sections_here, dtype=I32)
    allowed = (live_all[None, :] > 0) | (jnp.arange(sections, dtype=I32)[None, :] == own[:, None])
    scores = jnp.where(allowed[None, :, :], scores, F32(-1e30))
    probs = jax.nn.softmax(scores, axis=-1).astype(BF16)
    attended = jnp.einsum("hqk,khd->qhd", probs, value_heads, preferred_element_type=F32)
    attended = attended.astype(BF16).reshape(sections_here, cols)
    terms = jnp.dot(attended, w_out, preferred_element_type=F32)
    combined = jnp.sum(spread(terms, "segment"), axis=0)
    return (section_in + combined).astype(BF16)


def solution(mesh):
    in_specs = (
        P("segment", "seq", None),
        P(),
        P(),
        P("seq"),
        P("seq", None),
        P(),
        P(None, "segment"),
        P(None, "segment"),
        P(None, "segment"),
        P("segment", None),
    )
    return jax.shard_map(
        shards, mesh=mesh, in_specs=in_specs, out_specs=P("seq", None), check_vma=False
    )
```

```python
import functools

import jax
import jax.numpy as jnp
from jax import lax
from jax.experimental import pallas as pl
from jax.experimental.pallas import tpu as pltpu
from jax.sharding import PartitionSpec as P

HEAD_DIM = 128
SLOTS = 16
DEAD = 2.0**100
F32 = jnp.float32
BF16 = jnp.bfloat16
I32 = jnp.int32


def iota(shape, dim):
    return lax.broadcasted_iota(I32, shape, dim)


def below(shape, dim, other):
    return (iota(shape, dim) < iota(shape, other)).astype(F32).astype(BF16)


def turn(row):
    count = row.shape[1]
    same = iota((count, count), 0) == iota((count, count), 1)
    return jnp.sum(jnp.where(same, row, 0), axis=1, keepdims=True)


def turn_back(col):
    count = col.shape[0]
    same = iota((count, count), 0) == iota((count, count), 1)
    return jnp.sum(jnp.where(same, col, 0), axis=0, keepdims=True)


def pool_kernel(groups, slots, peers, chunks, hidden, lens, secs, *refs):
    rows, places, (level, buf, sems) = refs[:groups], refs[groups : 2 * groups], refs[2 * groups :]
    docs, spans = lens.shape
    sections = places[0].shape[-1]
    toks, width = buf.shape
    step = width // chunks
    copies = [
        pltpu.make_async_copy(
            hidden.at[0, :, pl.ds(j * step, step)], buf.at[:, pl.ds(j * step, step)], sems.at[j]
        )
        for j in range(chunks)
    ]
    for copy in copies:
        copy.start()
    doc = lax.axis_index("segment")
    here = lax.axis_index("seq")
    tok0 = (here * toks).astype(F32)
    lengths = lens[...]
    high = (lengths >> 4).astype(F32).astype(BF16)
    low = (lengths & 15).astype(F32).astype(BF16)
    upto = (iota((spans, spans), 0) <= iota((spans, spans), 1)).astype(F32).astype(BF16)
    ends = 16.0 * jnp.dot(high, upto, preferred_element_type=F32)
    ends = ends + jnp.dot(low, upto, preferred_element_type=F32)
    starts = ends - lengths.astype(F32)

    def pick(values):
        own = iota((docs, spans), 0) == doc
        return jnp.sum(jnp.where(own, values, 0), axis=0, keepdims=True)

    end_row = pick(ends)
    start_row = pick(starts)
    sec_row = pick(secs[...])
    section = iota((sections, 1), 0)
    hits = [section == secs[d : d + 1, :] for d in range(docs)]
    count = sum(hit.astype(F32) for hit in hits)
    count = jnp.sum(count, axis=1, keepdims=True)
    own = section == sec_row
    cover = (start_row < tok0 + toks) & (end_row > tok0)
    present = jnp.max((own & cover).astype(F32), axis=1, keepdims=True)
    ahead = iota((sections, sections), 1) < iota((sections, sections), 0)
    rank = jnp.sum(jnp.where(ahead, turn_back(present), 0.0), axis=1, keepdims=True)
    count_row = jnp.sum(jnp.where(own, count, 0.0), axis=0, keepdims=True)
    slot_row = jnp.sum(jnp.where(own, rank, 0.0), axis=0, keepdims=True)
    weight = 1.0 / jnp.maximum((end_row - start_row) * count_row, 1.0)
    every = groups * slots
    chosen = jnp.where(slot_row == iota((every, spans), 0).astype(F32), weight, 0.0)
    coarse = chosen.astype(BF16)
    fine = (chosen - coarse.astype(F32)).astype(BF16)
    at = tok0 + iota((1, toks), 1).astype(F32)
    inside = (turn(start_row) <= at) & (turn(end_row) > at)
    inside = inside.astype(F32).astype(BF16)
    picked = jnp.dot(jnp.concatenate([coarse, fine], axis=0), inside, preferred_element_type=F32)
    picked = picked.astype(BF16)

    peer_width = width // peers

    def work(j):
        copies[j].wait()
        part = jnp.dot(picked, buf[:, j * step : (j + 1) * step], preferred_element_type=F32)
        part = (part[:every] + part[every:]).astype(BF16)
        for i in range(step // peer_width):
            block = part[:, i * peer_width : (i + 1) * peer_width]
            for g in range(groups):
                rows[g][j * (step // peer_width) + i] = block[g * slots : (g + 1) * slots]

    for j in range(chunks // 2):
        work(j)

    edge = (iota((peers, 1), 0) * toks).astype(F32)
    before = below((sections, sections), 0, 1)

    def seen(start, end, hit):
        cover = ((start < edge + toks) & (end > edge)).astype(F32).astype(BF16)
        hit = hit.astype(F32).astype(BF16)
        found = lax.dot_general(cover, hit, (((1,), (1,)), ((), ())), preferred_element_type=F32)
        return (found > 0.0).astype(F32)

    mine = seen(start_row, end_row, own)
    order = jnp.dot(mine.astype(BF16), before, preferred_element_type=F32)
    order = jnp.where(mine > 0.0, order, -1.0)
    for q in range(peers):
        for g in range(groups):
            spot = (iota((slots, sections), 0) + g * slots).astype(F32)
            places[g][q] = (order[q : q + 1, :] == spot).astype(F32).astype(BF16)
    worst = jnp.zeros((peers, 1), F32)
    for d in range(docs):
        held = seen(starts[d : d + 1, :], ends[d : d + 1, :], hits[d])
        worst = jnp.maximum(worst, jnp.sum(held, axis=1, keepdims=True))
    worst = jnp.max(worst)
    level[0, 0] = (worst > slots).astype(I32) + (worst > 2 * slots).astype(I32)

    for j in range(chunks // 2, chunks):
        work(j)


def pool(hidden, span_lengths, section_of, groups, slots, peers, sections):
    toks, width = hidden.shape[1:]
    chunks = 16
    vmem = pl.BlockSpec(memory_space=pltpu.VMEM)
    out = pl.pallas_call(
        functools.partial(pool_kernel, groups, slots, peers, chunks),
        out_shape=(
            *[jax.ShapeDtypeStruct((peers, slots, width // peers), BF16)] * groups,
            *[jax.ShapeDtypeStruct((peers, slots, sections), BF16)] * groups,
            jax.ShapeDtypeStruct((1, 1), I32),
        ),
        in_specs=[pl.BlockSpec(memory_space=pl.ANY), vmem, vmem],
        out_specs=(*[vmem] * (2 * groups), pl.BlockSpec(memory_space=pltpu.SMEM)),
        scratch_shapes=[pltpu.VMEM((toks, width), BF16), pltpu.SemaphoreType.DMA((chunks,))],
        compiler_params=pltpu.CompilerParams(vmem_limit_bytes=50 * 1024 * 1024),
        name="pool",
    )(hidden, span_lengths, section_of)
    return out[:groups], out[groups : 2 * groups], out[-1]


def regroup(rows, place):
    got = lax.all_to_all(rows, "seq", 0, 0, tiled=True)
    got = got.reshape(-1, got.shape[-1])
    place = place.reshape(-1, place.shape[-1])
    pooled = lax.dot_general(place, got, (((0,), (0,)), ((), ())), preferred_element_type=F32)
    return pooled.astype(BF16)


def from_segments(block):
    size = lax.axis_size("segment")
    others = [
        lax.ppermute(block, "segment", [(i, (i + k) % size) for i in range(size)])
        for k in range(1, size)
    ]
    return [block, *others]


def project_kernel(pooled, w_in, _, out, wide):
    here = out.shape[1]
    wide[...] = jnp.dot(pooled[...], w_in[...], preferred_element_type=F32)
    for q in range(out.shape[0]):
        out[q] = wide[q * here : (q + 1) * here, :].astype(BF16)


def project(pooled, w_in, ahead, peers):
    sections, width = pooled.shape[0], w_in.shape[1]
    vmem = pl.BlockSpec(memory_space=pltpu.VMEM)
    return pl.pallas_call(
        project_kernel,
        out_shape=jax.ShapeDtypeStruct((peers, sections // peers, width), BF16),
        in_specs=[vmem] * 3,
        out_specs=vmem,
        scratch_shapes=[pltpu.VMEM((sections, width), F32)],
        compiler_params=pltpu.CompilerParams(vmem_limit_bytes=24 * 1024 * 1024),
        name="project",
    )(pooled, w_in, ahead)


def add_kernel(got, _, out):
    total = got[0].astype(F32)
    for q in range(1, got.shape[0]):
        total = total + got[q].astype(F32)
    out[...] = total


def add_peers(got, ahead):
    vmem = pl.BlockSpec(memory_space=pltpu.VMEM)
    return pl.pallas_call(
        add_kernel,
        out_shape=jax.ShapeDtypeStruct(got.shape[1:], F32),
        in_specs=[vmem] * 2,
        out_specs=vmem,
        compiler_params=pltpu.CompilerParams(vmem_limit_bytes=24 * 1024 * 1024),
        name="add_peers",
    )(got, ahead)


def by_head(full, here):
    row = iota((full.shape[0], 1), 0) // here
    heads = full.shape[0] // here
    return sum(
        jnp.where(row == h, full[:, h * HEAD_DIM : (h + 1) * HEAD_DIM], 0.0) for h in range(heads)
    )


def keys_kernel(docs, *refs):
    got, refs = refs[:docs], refs[docs:]
    gain, w_query, w_key, w_value, live, section_in, query, own, sent, wide = refs
    here = got[0].shape[0]
    heads = w_query.shape[1] // HEAD_DIM
    total = got[0][...]
    for part in got[1:]:
        total = total + part[...]
    section_in[...] = total
    scale = lax.rsqrt(jnp.mean(total * total, axis=1, keepdims=True) + 1e-05)
    normed = total * scale * gain[...]
    for h in range(heads):
        wide[h * here : (h + 1) * here, :] = normed
    normed = wide[...].astype(BF16)

    def project(weight):
        full = jnp.dot(normed, weight[...], preferred_element_type=F32)
        return by_head(full, here)

    key = project(w_key)
    value = project(w_value)
    spot = lax.rem(iota((heads * here, 1), 0), here)
    alive = jnp.zeros((heads * here, 1), I32)
    for i in range(here):
        alive = jnp.where(spot == i, live[i], alive)
    alive = alive > 0
    flag = jnp.where(iota(key.shape, 1) == 0, F32(DEAD), 0.0)
    pair = jnp.concatenate([jnp.where(alive, key, flag), jnp.where(alive, value, 0.0)], axis=1)
    pair = pair.astype(BF16)
    for q in range(sent.shape[0]):
        sent[q] = pair
    own[...] = jnp.concatenate([key, value], axis=1).astype(BF16)
    query[...] = project(w_query).astype(BF16)


def attend_kernel(got, query, own, w_out, terms, wide):
    peers, rows, _ = got.shape
    here = terms.shape[0]
    heads = rows // here
    both = got[...].reshape(peers * rows, 2 * HEAD_DIM)
    keys, values = both[:, :HEAD_DIM], both[:, HEAD_DIM:]
    across = (((1,), (1,)), ((), ()))
    q = query[...]
    root = jnp.sqrt(F32(HEAD_DIM))
    scores = lax.dot_general(q, keys, across, preferred_element_type=F32) / root
    first = (iota(q.shape, 1) == 0).astype(F32).astype(BF16)
    mark = lax.dot_general(first, keys, across, preferred_element_type=F32)
    mine_key = own[:, :HEAD_DIM].astype(F32)
    mine_value = own[:, HEAD_DIM:].astype(F32)
    score = jnp.sum(q.astype(F32) * mine_key, axis=1, keepdims=True) / root
    lane = iota((1, peers * rows), 1)
    row = iota((rows, 1), 0)
    mine = lane == row + lax.axis_index("seq") * rows
    same = lax.rem(lane, rows) // here == row // here
    scores = jnp.where(mark > DEAD * 0.5, F32(-1e30), scores)
    scores = jnp.where(mine, score, scores)
    peak = jnp.max(jnp.where(same, scores, F32(-3e38)), axis=1, keepdims=True)
    probs = jnp.where(same, jnp.exp(scores - peak), 0.0)
    probs = (probs / jnp.sum(probs, axis=1, keepdims=True)).astype(BF16).astype(F32)
    alone = jnp.sum(jnp.where(mine, probs, 0.0), axis=1, keepdims=True)
    rest = jnp.where(mine, 0.0, probs).astype(BF16)
    attended = jnp.dot(rest, values, preferred_element_type=F32) + alone * mine_value
    spread_out = jnp.concatenate([attended] * heads, axis=1)
    block = iota((1, heads * HEAD_DIM), 1) // HEAD_DIM
    spread_out = jnp.where(block == row // here, spread_out, 0.0).astype(BF16)
    wide[...] = jnp.dot(spread_out, w_out[...], preferred_element_type=F32)
    term = wide[0:here, :]
    for h in range(1, heads):
        term = term + wide[h * here : (h + 1) * here, :]
    terms[...] = term


def make_keys(got, gain, w_query, w_key, w_value, live, peers):
    here, width = got[0].shape
    rows = w_query.shape[1] // HEAD_DIM * here
    vmem = pl.BlockSpec(memory_space=pltpu.VMEM)
    return pl.pallas_call(
        functools.partial(keys_kernel, len(got)),
        out_shape=(
            jax.ShapeDtypeStruct((here, width), F32),
            jax.ShapeDtypeStruct((rows, HEAD_DIM), BF16),
            jax.ShapeDtypeStruct((rows, 2 * HEAD_DIM), BF16),
            jax.ShapeDtypeStruct((peers, rows, 2 * HEAD_DIM), BF16),
        ),
        in_specs=[vmem] * (len(got) + 4) + [pl.BlockSpec(memory_space=pltpu.SMEM)],
        out_specs=(vmem,) * 4,
        scratch_shapes=[pltpu.VMEM((rows, width), F32)],
        compiler_params=pltpu.CompilerParams(vmem_limit_bytes=24 * 1024 * 1024),
        name="make_keys",
    )(*got, gain[None, :], w_query, w_key, w_value, live)


def attend(got, query, own, w_out, here):
    rows, width = query.shape[0], w_out.shape[1]
    vmem = pl.BlockSpec(memory_space=pltpu.VMEM)
    return pl.pallas_call(
        attend_kernel,
        out_shape=jax.ShapeDtypeStruct((here, width), F32),
        in_specs=[vmem] * 4,
        out_specs=vmem,
        scratch_shapes=[pltpu.VMEM((rows, width), F32)],
        compiler_params=pltpu.CompilerParams(vmem_limit_bytes=24 * 1024 * 1024),
        name="attend",
    )(got, query, own, w_out)


def shards(
    hidden, span_lengths, section_of, section_live, w_in, norm_gain, w_query, w_key, w_value, w_out
):
    peers = lax.axis_size("seq")
    sections_here = section_live.shape[0]
    sections = sections_here * peers
    rows, place, level = pool(hidden, span_lengths, section_of, 2, SLOTS, peers, sections)

    def few(_):
        return regroup(rows[0], place[0])

    def some(_):
        return regroup(jnp.concatenate(rows, axis=1), jnp.concatenate(place, axis=1))

    def many(_):
        all_rows, all_place, _ = pool(
            hidden, span_lengths, section_of, 1, sections, peers, sections
        )
        return regroup(all_rows[0], all_place[0])

    pooled = lax.switch(level[0, 0], (few, some, many), 0)
    projected = project(pooled, w_in, w_query, peers)
    projected = lax.all_to_all(projected, "seq", 0, 0, tiled=True)
    doc_in = add_peers(projected, w_key)
    section_in, query, own, sent = make_keys(
        from_segments(doc_in), norm_gain, w_query, w_key, w_value, section_live, peers
    )
    got = lax.all_to_all(sent, "seq", 0, 0, tiled=True)
    terms = attend(got, query, own, w_out, sections_here)
    combined = sum(from_segments(terms))
    return (section_in + combined).astype(BF16)


def solution(mesh):
    in_specs = (
        P("segment", "seq", None),
        P(),
        P(),
        P("seq"),
        P("seq", None),
        P(),
        P(None, "segment"),
        P(None, "segment"),
        P(None, "segment"),
        P("segment", None),
    )
    return jax.shard_map(
        shards, mesh=mesh, in_specs=in_specs, out_specs=P("seq", None), check_vma=False
    )
```

```python
import functools

import jax
import jax.numpy as jnp
from jax import lax
from jax.experimental import pallas as pl
from jax.experimental.pallas import tpu as pltpu
from jax.sharding import PartitionSpec as P

HEAD_DIM = 128
SLOTS = 16
DEAD = 2.0**100
F32 = jnp.float32
BF16 = jnp.bfloat16
I32 = jnp.int32


def iota(shape, dim):
    return lax.broadcasted_iota(I32, shape, dim)


def bits(mask):
    return mask.astype(F32).astype(BF16)


def across(left, right):
    return lax.dot_general(left, right, (((1,), (1,)), ((), ())), preferred_element_type=F32)


def section_at(place, sections, peers):
    half = sections // 2
    here = sections // peers
    core, left = place // half, lax.rem(place, half)
    return (2 * (left // here) + core) * here + lax.rem(left, here)


def pool_kernel(groups, slots, peers, chunks, hidden, lens_far, secs_far, *refs):
    rows, places, refs = refs[:groups], refs[groups : 2 * groups], refs[2 * groups :]
    level, buf, lens, secs, sems, near = refs
    tables = [
        pltpu.make_async_copy(lens_far, lens, near.at[0]),
        pltpu.make_async_copy(secs_far, secs, near.at[1]),
    ]
    for copy in tables:
        copy.start()
    docs, spans = lens.shape
    sections = places[0].shape[-1]
    toks, width = buf.shape
    step = width // chunks
    copies = [
        pltpu.make_async_copy(
            hidden.at[0, :, pl.ds(j * step, step)], buf.at[:, pl.ds(j * step, step)], sems.at[j]
        )
        for j in range(chunks)
    ]
    for copy in copies:
        copy.start()
    for copy in tables:
        copy.wait()
    doc = lax.axis_index("segment")
    here = lax.axis_index("seq")
    tok0 = (here * toks).astype(F32)
    lengths = lens[...]
    high = (lengths >> 4).astype(F32)
    low = (lengths & 15).astype(F32)
    upto = bits(iota((spans, spans), 1) <= iota((spans, spans), 0))
    ends = 16.0 * across(high.astype(BF16), upto) + across(low.astype(BF16), upto)
    starts = ends - lengths.astype(F32)

    def pick(values):
        own = iota((docs, spans), 0) == doc
        return jnp.sum(jnp.where(own, values, 0), axis=0, keepdims=True)

    end_row = pick(ends)
    start_row = pick(starts)
    sec_row = pick(secs[...])
    half = toks // 8
    halves = (half, spans)
    both = [jnp.broadcast_to(pick(part), halves).astype(BF16) for part in (high, low)]
    both = jnp.concatenate(both, axis=0)

    def down(mask):
        out = across(mask, both)
        return 16.0 * out[:, :half] + out[:, half:]

    end_col = down(upto)
    start_col = down(bits(iota((spans, spans), 1) < iota((spans, spans), 0)))
    section = section_at(iota((sections, 1), 0), sections, peers)
    hits = [bits(section == secs[d : d + 1, :]) for d in range(docs)]
    own = bits(section == sec_row)
    edge = (iota((peers, 1), 0) * toks).astype(F32)

    def seen(start, end, hit):
        cover = bits((start < edge + toks) & (end > edge))
        return (across(cover, hit) > 0.0).astype(F32)

    mine = seen(start_row, end_row, own)
    before = bits(iota((sections, sections), 0) < iota((sections, sections), 1))
    order = jnp.dot(mine.astype(BF16), before, preferred_element_type=F32)
    order = jnp.where(mine > 0.0, order, -1.0)
    rank = jnp.sum(jnp.where(iota(order.shape, 0) == here, order, 0.0), axis=0, keepdims=True)
    ones = jnp.full((8, spans), 1.0, BF16)
    count = sum(across(ones, hit) for hit in hits)
    many = jnp.floor(count * (1.0 / 256.0))
    few = count - 256.0 * many

    def per_span(values):
        return jnp.dot(values.astype(BF16), own, preferred_element_type=F32)[:1]

    slot_row = per_span(jnp.broadcast_to(rank, (8, sections)))
    count_row = 256.0 * per_span(many) + per_span(few)
    weight = 1.0 / jnp.maximum((end_row - start_row) * count_row, 1.0)
    every = groups * slots
    chosen = jnp.where(slot_row == iota((every, spans), 0).astype(F32), weight, 0.0)
    coarse = chosen.astype(BF16)
    fine = (chosen - coarse.astype(F32)).astype(BF16)
    split = jnp.concatenate([coarse, fine], axis=0)
    picked = []
    for t in range(toks // half):
        at = tok0 + (t * half + iota((1, half), 1)).astype(F32)
        inside = bits((start_col <= at) & (end_col > at))
        picked.append(jnp.dot(split, inside, preferred_element_type=F32).astype(BF16))
    picked = jnp.concatenate(picked, axis=1)

    peer_width = width // peers

    def work(j):
        copies[j].wait()
        part = jnp.dot(picked, buf[:, j * step : (j + 1) * step], preferred_element_type=F32)
        part = (part[:every] + part[every:]).astype(BF16)
        for i in range(step // peer_width):
            block = part[:, i * peer_width : (i + 1) * peer_width]
            for g in range(groups):
                rows[g][j * (step // peer_width) + i] = block[g * slots : (g + 1) * slots]

    for j in range(chunks // 2):
        work(j)

    for q in range(peers):
        for g in range(groups):
            spot = (iota((slots, sections), 0) + g * slots).astype(F32)
            places[g][q] = (order[q : q + 1, :] == spot).astype(F32).astype(BF16)
    worst = jnp.zeros((peers, 1), F32)
    for d in range(docs):
        held = seen(starts[d : d + 1, :], ends[d : d + 1, :], hits[d])
        worst = jnp.maximum(worst, jnp.sum(held, axis=1, keepdims=True))
    worst = jnp.max(worst)
    level[0, 0] = (worst > slots).astype(I32) + (worst > 2 * slots).astype(I32)

    for j in range(chunks // 2, chunks):
        work(j)


def pool(hidden, span_lengths, section_of, groups, slots, peers, sections):
    toks, width = hidden.shape[1:]
    chunks = 8
    vmem = pl.BlockSpec(memory_space=pltpu.VMEM)
    out = pl.pallas_call(
        functools.partial(pool_kernel, groups, slots, peers, chunks),
        out_shape=(
            *[jax.ShapeDtypeStruct((peers, slots, width // peers), BF16)] * groups,
            *[jax.ShapeDtypeStruct((peers, slots, sections), BF16)] * groups,
            jax.ShapeDtypeStruct((1, 1), I32),
        ),
        in_specs=[pl.BlockSpec(memory_space=pl.ANY)] * 3,
        out_specs=(*[vmem] * (2 * groups), pl.BlockSpec(memory_space=pltpu.SMEM)),
        scratch_shapes=[
            pltpu.VMEM((toks, width), BF16),
            pltpu.VMEM(span_lengths.shape, I32),
            pltpu.VMEM(section_of.shape, I32),
            pltpu.SemaphoreType.DMA((chunks,)),
            pltpu.SemaphoreType.DMA((2,)),
        ],
        compiler_params=pltpu.CompilerParams(vmem_limit_bytes=50 * 1024 * 1024),
        name="pool",
    )(hidden, span_lengths, section_of)
    return out[:groups], out[groups : 2 * groups], out[-1]


def regroup(rows, place):
    got = lax.all_to_all(rows, "seq", 0, 0, tiled=True)
    got = got.reshape(-1, got.shape[-1])
    place = place.reshape(-1, place.shape[-1])
    pooled = lax.dot_general(place, got, (((0,), (0,)), ((), ())), preferred_element_type=F32)
    return pooled.astype(BF16)


def from_segments(block):
    size = lax.axis_size("segment")
    others = [
        lax.ppermute(block, "segment", [(i, (i + k) % size) for i in range(size)])
        for k in range(1, size)
    ]
    return [block, *others]


def project_kernel(own, pair, w_in, w_pair, _, out, wide):
    here = out.shape[1]
    wide[...] = jnp.dot(own[...], w_in[...], preferred_element_type=F32) + jnp.dot(
        pair[...], w_pair[...], preferred_element_type=F32
    )
    for q in range(out.shape[0]):
        out[q] = wide[q * here : (q + 1) * here, :].astype(BF16)


def project(own, pair, w_in, w_pair, ahead, chips):
    sections, width = own.shape[0], w_in.shape[1]
    vmem = pl.BlockSpec(memory_space=pltpu.VMEM)
    return pl.pallas_call(
        project_kernel,
        out_shape=jax.ShapeDtypeStruct((chips, sections // chips, width), BF16),
        in_specs=[vmem] * 5,
        out_specs=vmem,
        scratch_shapes=[pltpu.VMEM((sections, width), F32)],
        compiler_params=pltpu.CompilerParams(vmem_limit_bytes=24 * 1024 * 1024),
        name="project",
    )(own, pair, w_in, w_pair, ahead)


def add_kernel(got, _, out):
    total = got[0].astype(F32)
    for q in range(1, got.shape[0]):
        total = total + got[q].astype(F32)
    out[...] = total


def add_peers(got, ahead):
    vmem = pl.BlockSpec(memory_space=pltpu.VMEM)
    return pl.pallas_call(
        add_kernel,
        out_shape=jax.ShapeDtypeStruct(got.shape[1:], F32),
        in_specs=[vmem] * 2,
        out_specs=vmem,
        compiler_params=pltpu.CompilerParams(vmem_limit_bytes=24 * 1024 * 1024),
        name="add_peers",
    )(got, ahead)


def by_head(full, here):
    row = iota((full.shape[0], 1), 0) // here
    heads = full.shape[0] // here
    return sum(
        jnp.where(row == h, full[:, h * HEAD_DIM : (h + 1) * HEAD_DIM], 0.0) for h in range(heads)
    )


def keys_kernel(docs, *refs):
    got, refs = refs[:docs], refs[docs:]
    gain, w_query, w_key, w_value, live, section_in, query, own, sent, wide = refs
    here = got[0].shape[0]
    heads = w_query.shape[1] // HEAD_DIM
    total = got[0][...]
    for part in got[1:]:
        total = total + part[...]
    section_in[...] = total
    scale = lax.rsqrt(jnp.mean(total * total, axis=1, keepdims=True) + 1e-05)
    normed = total * scale * gain[...]
    for h in range(heads):
        wide[h * here : (h + 1) * here, :] = normed
    normed = wide[...].astype(BF16)

    def project(weight):
        full = jnp.dot(normed, weight[...], preferred_element_type=F32)
        return by_head(full, here)

    key = project(w_key)
    value = project(w_value)
    spot = lax.rem(iota((heads * here, 1), 0), here)
    alive = jnp.zeros((heads * here, 1), I32)
    for i in range(here):
        alive = jnp.where(spot == i, live[i], alive)
    alive = alive > 0
    flag = jnp.where(iota(key.shape, 1) == 0, F32(DEAD), 0.0)
    pair = jnp.concatenate([jnp.where(alive, key, flag), jnp.where(alive, value, 0.0)], axis=1)
    pair = pair.astype(BF16)
    for q in range(sent.shape[0]):
        sent[q] = pair
    own[...] = jnp.concatenate([key, value], axis=1).astype(BF16)
    query[...] = project(w_query).astype(BF16)


def attend_kernel(got, query, own, w_out, terms, wide):
    peers, rows, _ = got.shape
    here = terms.shape[0]
    heads = rows // here
    both = got[...].reshape(peers * rows, 2 * HEAD_DIM)
    keys, values = both[:, :HEAD_DIM], both[:, HEAD_DIM:]
    q = query[...]
    root = jnp.sqrt(F32(HEAD_DIM))
    scores = across(q, keys) / root
    first = (iota(q.shape, 1) == 0).astype(F32).astype(BF16)
    mark = across(first, keys)
    mine_key = own[:, :HEAD_DIM].astype(F32)
    mine_value = own[:, HEAD_DIM:].astype(F32)
    score = jnp.sum(q.astype(F32) * mine_key, axis=1, keepdims=True) / root
    lane = iota((1, peers * rows), 1)
    row = iota((rows, 1), 0)
    mine = lane == row + lax.axis_index("seq") * rows
    same = lax.rem(lane, rows) // here == row // here
    scores = jnp.where(mark > DEAD * 0.5, F32(-1e30), scores)
    scores = jnp.where(mine, score, scores)
    peak = jnp.max(jnp.where(same, scores, F32(-3e38)), axis=1, keepdims=True)
    probs = jnp.where(same, jnp.exp(scores - peak), 0.0)
    probs = (probs / jnp.sum(probs, axis=1, keepdims=True)).astype(BF16).astype(F32)
    alone = jnp.sum(jnp.where(mine, probs, 0.0), axis=1, keepdims=True)
    rest = jnp.where(mine, 0.0, probs).astype(BF16)
    attended = jnp.dot(rest, values, preferred_element_type=F32) + alone * mine_value
    spread_out = jnp.concatenate([attended] * heads, axis=1)
    block = iota((1, heads * HEAD_DIM), 1) // HEAD_DIM
    spread_out = jnp.where(block == row // here, spread_out, 0.0).astype(BF16)
    wide[...] = jnp.dot(spread_out, w_out[...], preferred_element_type=F32)
    term = wide[0:here, :]
    for h in range(1, heads):
        term = term + wide[h * here : (h + 1) * here, :]
    terms[...] = term


def make_keys(got, gain, w_query, w_key, w_value, live, peers):
    here, width = got[0].shape
    rows = w_query.shape[1] // HEAD_DIM * here
    vmem = pl.BlockSpec(memory_space=pltpu.VMEM)
    return pl.pallas_call(
        functools.partial(keys_kernel, len(got)),
        out_shape=(
            jax.ShapeDtypeStruct((here, width), F32),
            jax.ShapeDtypeStruct((rows, HEAD_DIM), BF16),
            jax.ShapeDtypeStruct((rows, 2 * HEAD_DIM), BF16),
            jax.ShapeDtypeStruct((peers, rows, 2 * HEAD_DIM), BF16),
        ),
        in_specs=[vmem] * (len(got) + 4) + [pl.BlockSpec(memory_space=pltpu.SMEM)],
        out_specs=(vmem,) * 4,
        scratch_shapes=[pltpu.VMEM((rows, width), F32)],
        compiler_params=pltpu.CompilerParams(vmem_limit_bytes=24 * 1024 * 1024),
        name="make_keys",
    )(*got, gain[None, :], w_query, w_key, w_value, live)


def attend(got, query, own, w_out, here):
    rows, width = query.shape[0], w_out.shape[1]
    vmem = pl.BlockSpec(memory_space=pltpu.VMEM)
    return pl.pallas_call(
        attend_kernel,
        out_shape=jax.ShapeDtypeStruct((here, width), F32),
        in_specs=[vmem] * 4,
        out_specs=vmem,
        scratch_shapes=[pltpu.VMEM((rows, width), F32)],
        compiler_params=pltpu.CompilerParams(vmem_limit_bytes=24 * 1024 * 1024),
        name="attend",
    )(got, query, own, w_out)


def shards(
    hidden, span_lengths, section_of, section_live, w_in, norm_gain, w_query, w_key, w_value, w_out
):
    peers = lax.axis_size("seq")
    sections_here = section_live.shape[0]
    sections = sections_here * peers
    swap = [(i, i ^ 1) for i in range(peers)]
    w_pair = lax.ppermute(w_in, "seq", swap)
    rows, place, level = pool(hidden, span_lengths, section_of, 2, SLOTS, peers, sections)

    def few(_):
        return regroup(rows[0], place[0])

    def some(_):
        return regroup(jnp.concatenate(rows, axis=1), jnp.concatenate(place, axis=1))

    def many(_):
        all_rows, all_place, _ = pool(
            hidden, span_lengths, section_of, 1, sections, peers, sections
        )
        return regroup(all_rows[0], all_place[0])

    pooled = lax.switch(level[0, 0], (few, some, many), 0)
    chips = [[i for i in range(peers) if i % 2 == core] for core in range(2)]
    half = sections // 2
    core = lax.rem(lax.axis_index("seq"), 2)
    own = lax.dynamic_slice_in_dim(pooled, core * half, half, 0)
    give = lax.dynamic_slice_in_dim(pooled, (1 - core) * half, half, 0)
    pair = lax.ppermute(give, "seq", swap)
    projected = project(own, pair, w_in, w_pair, w_query, peers // 2)
    projected = lax.all_to_all(projected, "seq", 0, 0, axis_index_groups=chips, tiled=True)
    doc_in = add_peers(projected, w_key)
    section_in, query, own, sent = make_keys(
        from_segments(doc_in), norm_gain, w_query, w_key, w_value, section_live, peers
    )
    got = lax.all_to_all(sent, "seq", 0, 0, tiled=True)
    terms = attend(got, query, own, w_out, sections_here)
    combined = sum(from_segments(terms))
    return (section_in + combined).astype(BF16)


def solution(mesh):
    in_specs = (
        P("segment", "seq", None),
        P(),
        P(),
        P("seq"),
        P("seq", None),
        P(),
        P(None, "segment"),
        P(None, "segment"),
        P(None, "segment"),
        P("segment", None),
    )
    return jax.shard_map(
        shards, mesh=mesh, in_specs=in_specs, out_specs=P("seq", None), check_vma=False
    )
```

```python
import functools

import jax
import jax.numpy as jnp
from jax import lax
from jax.experimental import pallas as pl
from jax.experimental.pallas import tpu as pltpu
from jax.sharding import PartitionSpec as P

HEAD_DIM = 128
SLOTS = 16
DEAD = 2.0**100
F32 = jnp.float32
BF16 = jnp.bfloat16
I32 = jnp.int32


def iota(shape, dim):
    return lax.broadcasted_iota(I32, shape, dim)


def below(shape, dim, other):
    return (iota(shape, dim) < iota(shape, other)).astype(F32).astype(BF16)


def turn(row):
    count = row.shape[1]
    same = iota((count, count), 0) == iota((count, count), 1)
    return jnp.sum(jnp.where(same, row, 0), axis=1, keepdims=True)


def turn_back(col):
    count = col.shape[0]
    same = iota((count, count), 0) == iota((count, count), 1)
    return jnp.sum(jnp.where(same, col, 0), axis=0, keepdims=True)


def bits(mask):
    return mask.astype(F32).astype(BF16)


def across(left, right):
    return lax.dot_general(left, right, (((1,), (1,)), ((), ())), preferred_element_type=F32)


def section_at(place, sections, peers):
    half, here = sections // 2, sections // peers
    core = (place >= half).astype(I32)
    left = place - core * half
    chip = left >> (here.bit_length() - 1)
    return left + (chip + core) * here


def pool_kernel(groups, slots, peers, chunks, hidden, lens, secs, *refs):
    rows, places, (level, buf, sems) = refs[:groups], refs[groups : 2 * groups], refs[2 * groups :]
    docs, spans = lens.shape
    sections = places[0].shape[-1]
    toks, width = buf.shape
    step = width // chunks
    copies = [
        pltpu.make_async_copy(
            hidden.at[0, :, pl.ds(j * step, step)], buf.at[:, pl.ds(j * step, step)], sems.at[j]
        )
        for j in range(chunks)
    ]
    for copy in copies:
        copy.start()
    doc = lax.axis_index("segment")
    here = lax.axis_index("seq")
    tok0 = (here * toks).astype(F32)
    lengths = lens[...]
    high = (lengths >> 4).astype(F32).astype(BF16)
    low = (lengths & 15).astype(F32).astype(BF16)
    upto = (iota((spans, spans), 0) <= iota((spans, spans), 1)).astype(F32).astype(BF16)
    ends = 16.0 * jnp.dot(high, upto, preferred_element_type=F32)
    ends = ends + jnp.dot(low, upto, preferred_element_type=F32)
    starts = ends - lengths.astype(F32)

    def pick(values):
        own = iota((docs, spans), 0) == doc
        return jnp.sum(jnp.where(own, values, 0), axis=0, keepdims=True)

    end_row = pick(ends)
    start_row = pick(starts)
    sec_row = pick(secs[...])
    section = section_at(iota((sections, 1), 0), sections, peers)
    hits = [section == secs[d : d + 1, :] for d in range(docs)]
    count = sum(hit.astype(F32) for hit in hits)
    count = jnp.sum(count, axis=1, keepdims=True)
    own = section == sec_row
    cover = (start_row < tok0 + toks) & (end_row > tok0)
    present = jnp.max((own & cover).astype(F32), axis=1, keepdims=True)
    ahead = iota((sections, sections), 1) < iota((sections, sections), 0)
    rank = jnp.sum(jnp.where(ahead, turn_back(present), 0.0), axis=1, keepdims=True)
    count_row = jnp.sum(jnp.where(own, count, 0.0), axis=0, keepdims=True)
    slot_row = jnp.sum(jnp.where(own, rank, 0.0), axis=0, keepdims=True)
    weight = 1.0 / jnp.maximum((end_row - start_row) * count_row, 1.0)
    every = groups * slots
    chosen = jnp.where(slot_row == iota((every, spans), 0).astype(F32), weight, 0.0)
    coarse = chosen.astype(BF16)
    fine = (chosen - coarse.astype(F32)).astype(BF16)
    at = tok0 + iota((1, toks), 1).astype(F32)
    inside = (turn(start_row) <= at) & (turn(end_row) > at)
    inside = inside.astype(F32).astype(BF16)
    picked = jnp.dot(jnp.concatenate([coarse, fine], axis=0), inside, preferred_element_type=F32)
    picked = picked.astype(BF16)

    peer_width = width // peers

    def work(j):
        copies[j].wait()
        part = jnp.dot(picked, buf[:, j * step : (j + 1) * step], preferred_element_type=F32)
        part = (part[:every] + part[every:]).astype(BF16)
        for i in range(step // peer_width):
            block = part[:, i * peer_width : (i + 1) * peer_width]
            for g in range(groups):
                rows[g][j * (step // peer_width) + i] = block[g * slots : (g + 1) * slots]

    for j in range(chunks // 2):
        work(j)

    edge = (iota((peers, 1), 0) * toks).astype(F32)
    before = below((sections, sections), 0, 1)

    def seen(start, end, hit):
        cover = ((start < edge + toks) & (end > edge)).astype(F32).astype(BF16)
        hit = hit.astype(F32).astype(BF16)
        found = lax.dot_general(cover, hit, (((1,), (1,)), ((), ())), preferred_element_type=F32)
        return (found > 0.0).astype(F32)

    mine = seen(start_row, end_row, own)
    order = jnp.dot(mine.astype(BF16), before, preferred_element_type=F32)
    order = jnp.where(mine > 0.0, order, -1.0)
    for q in range(peers):
        for g in range(groups):
            spot = (iota((slots, sections), 0) + g * slots).astype(F32)
            places[g][q] = (order[q : q + 1, :] == spot).astype(F32).astype(BF16)
    worst = jnp.zeros((peers, 1), F32)
    for d in range(docs):
        held = seen(starts[d : d + 1, :], ends[d : d + 1, :], hits[d])
        worst = jnp.maximum(worst, jnp.sum(held, axis=1, keepdims=True))
    worst = jnp.max(worst)
    level[0, 0] = (worst > slots).astype(I32) + (worst > 2 * slots).astype(I32)

    for j in range(chunks // 2, chunks):
        work(j)


def pool(hidden, span_lengths, section_of, groups, slots, peers, sections):
    toks, width = hidden.shape[1:]
    chunks = 8
    vmem = pl.BlockSpec(memory_space=pltpu.VMEM)
    out = pl.pallas_call(
        functools.partial(pool_kernel, groups, slots, peers, chunks),
        out_shape=(
            *[jax.ShapeDtypeStruct((peers, slots, width // peers), BF16)] * groups,
            *[jax.ShapeDtypeStruct((peers, slots, sections), BF16)] * groups,
            jax.ShapeDtypeStruct((1, 1), I32),
        ),
        in_specs=[pl.BlockSpec(memory_space=pl.ANY), vmem, vmem],
        out_specs=(*[vmem] * (2 * groups), pl.BlockSpec(memory_space=pltpu.SMEM)),
        scratch_shapes=[pltpu.VMEM((toks, width), BF16), pltpu.SemaphoreType.DMA((chunks,))],
        compiler_params=pltpu.CompilerParams(vmem_limit_bytes=48 * 1024 * 1024),
        name="pool",
    )(hidden, span_lengths, section_of)
    return out[:groups], out[groups : 2 * groups], out[-1]


def regroup(rows, place):
    got = lax.all_to_all(rows, "seq", 0, 0, tiled=True)
    got = got.reshape(-1, got.shape[-1])
    place = place.reshape(-1, place.shape[-1])
    pooled = lax.dot_general(place, got, (((0,), (0,)), ((), ())), preferred_element_type=F32)
    return pooled.astype(BF16)


def from_segments(block):
    size = lax.axis_size("segment")
    others = [
        lax.ppermute(block, "segment", [(i, (i + k) % size) for i in range(size)])
        for k in range(1, size)
    ]
    return [block, *others]


def project_kernel(pooled, w_in, _, own, give):
    half = own.shape[0]
    core = lax.rem(lax.axis_index("seq"), 2)

    def rows(which):
        block = pooled[pl.ds(pl.multiple_of(which * half, half), half), :]
        return jnp.dot(block, w_in[...], preferred_element_type=F32)

    give[...] = rows(1 - core).astype(BF16)
    own[...] = rows(core)


def project(pooled, w_in, ahead):
    half, width = pooled.shape[0] // 2, w_in.shape[1]
    vmem = pl.BlockSpec(memory_space=pltpu.VMEM)
    return pl.pallas_call(
        project_kernel,
        out_shape=(
            jax.ShapeDtypeStruct((half, width), F32),
            jax.ShapeDtypeStruct((half, width), BF16),
        ),
        in_specs=[vmem] * 3,
        out_specs=(vmem, vmem),
        compiler_params=pltpu.CompilerParams(vmem_limit_bytes=24 * 1024 * 1024),
        name="project",
    )(pooled, w_in, ahead)


def merge_kernel(own, pair, out, wide):
    here = out.shape[1]
    wide[...] = own[...] + pair[...].astype(F32)
    for q in range(out.shape[0]):
        out[q] = wide[q * here : (q + 1) * here, :].astype(BF16)


def merge(own, pair, chips):
    half, width = own.shape
    vmem = pl.BlockSpec(memory_space=pltpu.VMEM)
    return pl.pallas_call(
        merge_kernel,
        out_shape=jax.ShapeDtypeStruct((chips, half // chips, width), BF16),
        in_specs=[vmem] * 2,
        out_specs=vmem,
        scratch_shapes=[pltpu.VMEM((half, width), F32)],
        compiler_params=pltpu.CompilerParams(vmem_limit_bytes=24 * 1024 * 1024),
        name="merge",
    )(own, pair)


def add_kernel(got, _, out):
    total = got[0].astype(F32)
    for q in range(1, got.shape[0]):
        total = total + got[q].astype(F32)
    out[...] = total


def add_peers(got, ahead):
    vmem = pl.BlockSpec(memory_space=pltpu.VMEM)
    return pl.pallas_call(
        add_kernel,
        out_shape=jax.ShapeDtypeStruct(got.shape[1:], F32),
        in_specs=[vmem] * 2,
        out_specs=vmem,
        compiler_params=pltpu.CompilerParams(vmem_limit_bytes=24 * 1024 * 1024),
        name="add_peers",
    )(got, ahead)


def by_head(full, here):
    row = iota((full.shape[0], 1), 0) // here
    heads = full.shape[0] // here
    return sum(
        jnp.where(row == h, full[:, h * HEAD_DIM : (h + 1) * HEAD_DIM], 0.0) for h in range(heads)
    )


def keys_kernel(docs, *refs):
    got, refs = refs[:docs], refs[docs:]
    gain, w_query, w_key, w_value, live, section_in, query, own, sent, wide = refs
    here = got[0].shape[0]
    heads = w_query.shape[1] // HEAD_DIM
    total = got[0][...]
    for part in got[1:]:
        total = total + part[...]
    section_in[...] = total
    scale = lax.rsqrt(jnp.mean(total * total, axis=1, keepdims=True) + 1e-05)
    normed = total * scale * gain[...]
    for h in range(heads):
        wide[h * here : (h + 1) * here, :] = normed
    normed = wide[...].astype(BF16)

    def project(weight):
        full = jnp.dot(normed, weight[...], preferred_element_type=F32)
        return by_head(full, here)

    key = project(w_key)
    value = project(w_value)
    spot = lax.rem(iota((heads * here, 1), 0), here)
    alive = jnp.zeros((heads * here, 1), I32)
    for i in range(here):
        alive = jnp.where(spot == i, live[i], alive)
    alive = alive > 0
    flag = jnp.where(iota(key.shape, 1) == 0, F32(DEAD), 0.0)
    pair = jnp.concatenate([jnp.where(alive, key, flag), jnp.where(alive, value, 0.0)], axis=1)
    pair = pair.astype(BF16)
    for q in range(sent.shape[0]):
        sent[q] = pair
    own[...] = jnp.concatenate([key, value], axis=1).astype(BF16)
    query[...] = project(w_query).astype(BF16)


def attend_kernel(got, query, own, w_out, terms, wide):
    peers, rows, _ = got.shape
    here = terms.shape[0]
    heads = rows // here
    both = got[...].reshape(peers * rows, 2 * HEAD_DIM)
    keys, values = both[:, :HEAD_DIM], both[:, HEAD_DIM:]
    q = query[...]
    root = jnp.sqrt(F32(HEAD_DIM))
    scores = across(q, keys) / root
    first = (iota(q.shape, 1) == 0).astype(F32).astype(BF16)
    mark = across(first, keys)
    mine_key = own[:, :HEAD_DIM].astype(F32)
    mine_value = own[:, HEAD_DIM:].astype(F32)
    score = jnp.sum(q.astype(F32) * mine_key, axis=1, keepdims=True) / root
    lane = iota((1, peers * rows), 1)
    row = iota((rows, 1), 0)
    mine = lane == row + lax.axis_index("seq") * rows
    same = lax.rem(lane, rows) // here == row // here
    scores = jnp.where(mark > DEAD * 0.5, F32(-1e30), scores)
    scores = jnp.where(mine, score, scores)
    peak = jnp.max(jnp.where(same, scores, F32(-3e38)), axis=1, keepdims=True)
    probs = jnp.where(same, jnp.exp(scores - peak), 0.0)
    probs = (probs / jnp.sum(probs, axis=1, keepdims=True)).astype(BF16).astype(F32)
    alone = jnp.sum(jnp.where(mine, probs, 0.0), axis=1, keepdims=True)
    rest = jnp.where(mine, 0.0, probs).astype(BF16)
    attended = jnp.dot(rest, values, preferred_element_type=F32) + alone * mine_value
    spread_out = jnp.concatenate([attended] * heads, axis=1)
    block = iota((1, heads * HEAD_DIM), 1) // HEAD_DIM
    spread_out = jnp.where(block == row // here, spread_out, 0.0).astype(BF16)
    wide[...] = jnp.dot(spread_out, w_out[...], preferred_element_type=F32)
    term = wide[0:here, :]
    for h in range(1, heads):
        term = term + wide[h * here : (h + 1) * here, :]
    terms[...] = term


def make_keys(got, gain, w_query, w_key, w_value, live, peers):
    here, width = got[0].shape
    rows = w_query.shape[1] // HEAD_DIM * here
    vmem = pl.BlockSpec(memory_space=pltpu.VMEM)
    return pl.pallas_call(
        functools.partial(keys_kernel, len(got)),
        out_shape=(
            jax.ShapeDtypeStruct((here, width), F32),
            jax.ShapeDtypeStruct((rows, HEAD_DIM), BF16),
            jax.ShapeDtypeStruct((rows, 2 * HEAD_DIM), BF16),
            jax.ShapeDtypeStruct((peers, rows, 2 * HEAD_DIM), BF16),
        ),
        in_specs=[vmem] * (len(got) + 4) + [pl.BlockSpec(memory_space=pltpu.SMEM)],
        out_specs=(vmem,) * 4,
        scratch_shapes=[pltpu.VMEM((rows, width), F32)],
        compiler_params=pltpu.CompilerParams(vmem_limit_bytes=24 * 1024 * 1024),
        name="make_keys",
    )(*got, gain[None, :], w_query, w_key, w_value, live)


def attend(got, query, own, w_out, here):
    rows, width = query.shape[0], w_out.shape[1]
    vmem = pl.BlockSpec(memory_space=pltpu.VMEM)
    return pl.pallas_call(
        attend_kernel,
        out_shape=jax.ShapeDtypeStruct((here, width), F32),
        in_specs=[vmem] * 4,
        out_specs=vmem,
        scratch_shapes=[pltpu.VMEM((rows, width), F32)],
        compiler_params=pltpu.CompilerParams(vmem_limit_bytes=24 * 1024 * 1024),
        name="attend",
    )(got, query, own, w_out)


def shards(
    hidden, span_lengths, section_of, section_live, w_in, norm_gain, w_query, w_key, w_value, w_out
):
    peers = lax.axis_size("seq")
    sections_here = section_live.shape[0]
    sections = sections_here * peers
    swap = [(i, i ^ 1) for i in range(peers)]
    rows, place, level = pool(hidden, span_lengths, section_of, 2, SLOTS, peers, sections)

    def few(_):
        return regroup(rows[0], place[0])

    def some(_):
        return regroup(jnp.concatenate(rows, axis=1), jnp.concatenate(place, axis=1))

    def many(_):
        all_rows, all_place, _ = pool(
            hidden, span_lengths, section_of, 1, sections, peers, sections
        )
        return regroup(all_rows[0], all_place[0])

    pooled = lax.switch(level[0, 0], (few, some, many), 0)
    chips = [[i for i in range(peers) if i % 2 == core] for core in range(2)]
    own, give = project(pooled, w_in, w_query)
    projected = merge(own, lax.ppermute(give, "seq", swap), peers // 2)
    projected = lax.all_to_all(projected, "seq", 0, 0, axis_index_groups=chips, tiled=True)
    doc_in = add_peers(projected, w_key)
    section_in, query, own, sent = make_keys(
        from_segments(doc_in), norm_gain, w_query, w_key, w_value, section_live, peers
    )
    got = lax.all_to_all(sent, "seq", 0, 0, tiled=True)
    terms = attend(got, query, own, w_out, sections_here)
    combined = sum(from_segments(terms))
    return (section_in + combined).astype(BF16)


def solution(mesh):
    in_specs = (
        P("segment", "seq", None),
        P(),
        P(),
        P("seq"),
        P("seq", None),
        P(),
        P(None, "segment"),
        P(None, "segment"),
        P(None, "segment"),
        P("segment", None),
    )
    return jax.shard_map(
        shards, mesh=mesh, in_specs=in_specs, out_specs=P("seq", None), check_vma=False
    )
```

```python
import functools

import jax
import jax.numpy as jnp
from jax import lax
from jax.experimental import pallas as pl
from jax.experimental.pallas import tpu as pltpu
from jax.sharding import PartitionSpec as P

HEAD_DIM = 128
SLOTS = 16
DEAD = 2.0**100
F32 = jnp.float32
BF16 = jnp.bfloat16
I32 = jnp.int32


def iota(shape, dim):
    return lax.broadcasted_iota(I32, shape, dim)


def below(shape, dim, other):
    return (iota(shape, dim) < iota(shape, other)).astype(F32).astype(BF16)


def turn(row):
    count = row.shape[1]
    same = iota((count, count), 0) == iota((count, count), 1)
    return jnp.sum(jnp.where(same, row, 0), axis=1, keepdims=True)


def turn_back(col):
    count = col.shape[0]
    same = iota((count, count), 0) == iota((count, count), 1)
    return jnp.sum(jnp.where(same, col, 0), axis=0, keepdims=True)


def bits(mask):
    return mask.astype(F32).astype(BF16)


def across(left, right):
    return lax.dot_general(left, right, (((1,), (1,)), ((), ())), preferred_element_type=F32)


def section_at(place, sections, peers):
    half, here = sections // 2, sections // peers
    core = (place >= half).astype(I32)
    left = place - core * half
    chip = left >> (here.bit_length() - 1)
    return left + (chip + core) * here


def pool_kernel(groups, slots, peers, chunks, hidden, lens, secs, *refs):
    rows, places, (level, buf, sems) = refs[:groups], refs[groups : 2 * groups], refs[2 * groups :]
    docs, spans = lens.shape
    sections = places[0].shape[-1]
    toks, width = buf.shape
    step = width // chunks
    copies = [
        pltpu.make_async_copy(
            hidden.at[0, :, pl.ds(j * step, step)], buf.at[:, pl.ds(j * step, step)], sems.at[j]
        )
        for j in range(chunks)
    ]
    for copy in copies:
        copy.start()
    doc = lax.axis_index("segment")
    here = lax.axis_index("seq")
    tok0 = (here * toks).astype(F32)
    lengths = lens[...]
    high = (lengths >> 4).astype(F32).astype(BF16)
    low = (lengths & 15).astype(F32).astype(BF16)
    upto = (iota((spans, spans), 0) <= iota((spans, spans), 1)).astype(F32).astype(BF16)
    ends = 16.0 * jnp.dot(high, upto, preferred_element_type=F32)
    ends = ends + jnp.dot(low, upto, preferred_element_type=F32)
    starts = ends - lengths.astype(F32)

    def pick(values):
        own = iota((docs, spans), 0) == doc
        return jnp.sum(jnp.where(own, values, 0), axis=0, keepdims=True)

    end_row = pick(ends)
    start_row = pick(starts)
    sec_row = pick(secs[...])
    section = section_at(iota((sections, 1), 0), sections, peers)
    hits = [section == secs[d : d + 1, :] for d in range(docs)]
    count = sum(hit.astype(F32) for hit in hits)
    count = jnp.sum(count, axis=1, keepdims=True)
    own = section == sec_row
    cover = (start_row < tok0 + toks) & (end_row > tok0)
    present = jnp.max((own & cover).astype(F32), axis=1, keepdims=True)
    ahead = iota((sections, sections), 1) < iota((sections, sections), 0)
    rank = jnp.sum(jnp.where(ahead, turn_back(present), 0.0), axis=1, keepdims=True)
    count_row = jnp.sum(jnp.where(own, count, 0.0), axis=0, keepdims=True)
    slot_row = jnp.sum(jnp.where(own, rank, 0.0), axis=0, keepdims=True)
    weight = 1.0 / jnp.maximum((end_row - start_row) * count_row, 1.0)
    every = groups * slots
    chosen = jnp.where(slot_row == iota((every, spans), 0).astype(F32), weight, 0.0)
    coarse = chosen.astype(BF16)
    fine = (chosen - coarse.astype(F32)).astype(BF16)
    at = tok0 + iota((1, toks), 1).astype(F32)
    inside = (turn(start_row) <= at) & (turn(end_row) > at)
    inside = inside.astype(F32).astype(BF16)
    picked = jnp.dot(jnp.concatenate([coarse, fine], axis=0), inside, preferred_element_type=F32)
    picked = picked.astype(BF16)

    peer_width = width // peers

    def work(j):
        copies[j].wait()
        part = jnp.dot(picked, buf[:, j * step : (j + 1) * step], preferred_element_type=F32)
        part = (part[:every] + part[every:]).astype(BF16)
        for i in range(step // peer_width):
            block = part[:, i * peer_width : (i + 1) * peer_width]
            for g in range(groups):
                rows[g][j * (step // peer_width) + i] = block[g * slots : (g + 1) * slots]

    for j in range(chunks // 2):
        work(j)

    edge = (iota((peers, 1), 0) * toks).astype(F32)
    before = below((sections, sections), 0, 1)

    def seen(start, end, hit):
        cover = ((start < edge + toks) & (end > edge)).astype(F32).astype(BF16)
        hit = hit.astype(F32).astype(BF16)
        found = lax.dot_general(cover, hit, (((1,), (1,)), ((), ())), preferred_element_type=F32)
        return (found > 0.0).astype(F32)

    mine = seen(start_row, end_row, own)
    order = jnp.dot(mine.astype(BF16), before, preferred_element_type=F32)
    order = jnp.where(mine > 0.0, order, -1.0)
    for q in range(peers):
        for g in range(groups):
            spot = (iota((slots, sections), 0) + g * slots).astype(F32)
            places[g][q] = (order[q : q + 1, :] == spot).astype(F32).astype(BF16)
    worst = jnp.zeros((peers, 1), F32)
    for d in range(docs):
        held = seen(starts[d : d + 1, :], ends[d : d + 1, :], hits[d])
        worst = jnp.maximum(worst, jnp.sum(held, axis=1, keepdims=True))
    worst = jnp.max(worst, axis=0, keepdims=True)
    tier = (worst > slots).astype(I32) + (worst > 2 * slots).astype(I32)
    level[...] = jnp.broadcast_to(tier, level.shape)

    for j in range(chunks // 2, chunks):
        work(j)


def pool(hidden, span_lengths, section_of, groups, slots, peers, sections):
    toks, width = hidden.shape[1:]
    chunks = 8
    vmem = pl.BlockSpec(memory_space=pltpu.VMEM)
    out = pl.pallas_call(
        functools.partial(pool_kernel, groups, slots, peers, chunks),
        out_shape=(
            *[jax.ShapeDtypeStruct((peers, slots, width // peers), BF16)] * groups,
            *[jax.ShapeDtypeStruct((peers, slots, sections), BF16)] * groups,
            jax.ShapeDtypeStruct((1, 128), I32),
        ),
        in_specs=[pl.BlockSpec(memory_space=pl.ANY), vmem, vmem],
        out_specs=(*[vmem] * (2 * groups), vmem),
        scratch_shapes=[pltpu.VMEM((toks, width), BF16), pltpu.SemaphoreType.DMA((chunks,))],
        compiler_params=pltpu.CompilerParams(vmem_limit_bytes=48 * 1024 * 1024),
        name="pool",
    )(hidden, span_lengths, section_of)
    return out[:groups], out[groups : 2 * groups], out[-1]


def regroup(rows, place):
    got = lax.all_to_all(rows, "seq", 0, 0, tiled=True)
    got = got.reshape(-1, got.shape[-1])
    place = place.reshape(-1, place.shape[-1])
    pooled = lax.dot_general(place, got, (((0,), (0,)), ((), ())), preferred_element_type=F32)
    return pooled.astype(BF16)


def from_segments(block):
    size = lax.axis_size("segment")
    others = [
        lax.ppermute(block, "segment", [(i, (i + k) % size) for i in range(size)])
        for k in range(1, size)
    ]
    return [block, *others]


def project_kernel(pooled, w_in, _, own, give):
    half = own.shape[0]
    core = lax.rem(lax.axis_index("seq"), 2)

    def rows(which):
        block = pooled[pl.ds(pl.multiple_of(which * half, half), half), :]
        return jnp.dot(block, w_in[...], preferred_element_type=F32)

    give[...] = rows(1 - core).astype(BF16)
    own[...] = rows(core)


def project(pooled, w_in, ahead):
    half, width = pooled.shape[0] // 2, w_in.shape[1]
    vmem = pl.BlockSpec(memory_space=pltpu.VMEM)
    return pl.pallas_call(
        project_kernel,
        out_shape=(
            jax.ShapeDtypeStruct((half, width), F32),
            jax.ShapeDtypeStruct((half, width), BF16),
        ),
        in_specs=[vmem] * 3,
        out_specs=(vmem, vmem),
        compiler_params=pltpu.CompilerParams(vmem_limit_bytes=24 * 1024 * 1024),
        name="project",
    )(pooled, w_in, ahead)


def merge_kernel(own, pair, out, wide):
    here = out.shape[1]
    wide[...] = own[...] + pair[...].astype(F32)
    for q in range(out.shape[0]):
        out[q] = wide[q * here : (q + 1) * here, :].astype(BF16)


def merge(own, pair, chips):
    half, width = own.shape
    vmem = pl.BlockSpec(memory_space=pltpu.VMEM)
    return pl.pallas_call(
        merge_kernel,
        out_shape=jax.ShapeDtypeStruct((chips, half // chips, width), BF16),
        in_specs=[vmem] * 2,
        out_specs=vmem,
        scratch_shapes=[pltpu.VMEM((half, width), F32)],
        compiler_params=pltpu.CompilerParams(vmem_limit_bytes=24 * 1024 * 1024),
        name="merge",
    )(own, pair)


def add_kernel(got, _, out):
    total = got[0].astype(F32)
    for q in range(1, got.shape[0]):
        total = total + got[q].astype(F32)
    out[...] = total


def add_peers(got, ahead):
    vmem = pl.BlockSpec(memory_space=pltpu.VMEM)
    return pl.pallas_call(
        add_kernel,
        out_shape=jax.ShapeDtypeStruct(got.shape[1:], F32),
        in_specs=[vmem] * 2,
        out_specs=vmem,
        compiler_params=pltpu.CompilerParams(vmem_limit_bytes=24 * 1024 * 1024),
        name="add_peers",
    )(got, ahead)


def by_head(full, here):
    row = iota((full.shape[0], 1), 0) // here
    heads = full.shape[0] // here
    return sum(
        jnp.where(row == h, full[:, h * HEAD_DIM : (h + 1) * HEAD_DIM], 0.0) for h in range(heads)
    )


def keys_kernel(docs, *refs):
    got, refs = refs[:docs], refs[docs:]
    gain, w_query, w_key, w_value, live, section_in, query, own, sent, wide = refs
    here = got[0].shape[0]
    heads = w_query.shape[1] // HEAD_DIM
    total = got[0][...]
    for part in got[1:]:
        total = total + part[...]
    section_in[...] = total
    scale = lax.rsqrt(jnp.mean(total * total, axis=1, keepdims=True) + 1e-05)
    normed = total * scale * gain[...]
    for h in range(heads):
        wide[h * here : (h + 1) * here, :] = normed
    normed = wide[...].astype(BF16)

    def project(weight):
        full = jnp.dot(normed, weight[...], preferred_element_type=F32)
        return by_head(full, here)

    key = project(w_key)
    value = project(w_value)
    spot = lax.rem(iota((heads * here, 1), 0), here)
    alive = jnp.zeros((heads * here, 1), I32)
    for i in range(here):
        alive = jnp.where(spot == i, live[i], alive)
    alive = alive > 0
    flag = jnp.where(iota(key.shape, 1) == 0, F32(DEAD), 0.0)
    pair = jnp.concatenate([jnp.where(alive, key, flag), jnp.where(alive, value, 0.0)], axis=1)
    pair = pair.astype(BF16)
    for q in range(sent.shape[0]):
        sent[q] = pair
    own[...] = jnp.concatenate([key, value], axis=1).astype(BF16)
    query[...] = project(w_query).astype(BF16)


def attend_kernel(got, query, own, w_out, terms, wide):
    peers, rows, _ = got.shape
    here = terms.shape[0]
    heads = rows // here
    both = got[...].reshape(peers * rows, 2 * HEAD_DIM)
    keys, values = both[:, :HEAD_DIM], both[:, HEAD_DIM:]
    q = query[...]
    root = jnp.sqrt(F32(HEAD_DIM))
    scores = across(q, keys) / root
    first = (iota(q.shape, 1) == 0).astype(F32).astype(BF16)
    mark = across(first, keys)
    mine_key = own[:, :HEAD_DIM].astype(F32)
    mine_value = own[:, HEAD_DIM:].astype(F32)
    score = jnp.sum(q.astype(F32) * mine_key, axis=1, keepdims=True) / root
    lane = iota((1, peers * rows), 1)
    row = iota((rows, 1), 0)
    mine = lane == row + lax.axis_index("seq") * rows
    same = lax.rem(lane, rows) // here == row // here
    scores = jnp.where(mark > DEAD * 0.5, F32(-1e30), scores)
    scores = jnp.where(mine, score, scores)
    peak = jnp.max(jnp.where(same, scores, F32(-3e38)), axis=1, keepdims=True)
    probs = jnp.where(same, jnp.exp(scores - peak), 0.0)
    probs = (probs / jnp.sum(probs, axis=1, keepdims=True)).astype(BF16).astype(F32)
    alone = jnp.sum(jnp.where(mine, probs, 0.0), axis=1, keepdims=True)
    rest = jnp.where(mine, 0.0, probs).astype(BF16)
    attended = jnp.dot(rest, values, preferred_element_type=F32) + alone * mine_value
    spread_out = jnp.concatenate([attended] * heads, axis=1)
    block = iota((1, heads * HEAD_DIM), 1) // HEAD_DIM
    spread_out = jnp.where(block == row // here, spread_out, 0.0).astype(BF16)
    wide[...] = jnp.dot(spread_out, w_out[...], preferred_element_type=F32)
    term = wide[0:here, :]
    for h in range(1, heads):
        term = term + wide[h * here : (h + 1) * here, :]
    terms[...] = term


def make_keys(got, gain, w_query, w_key, w_value, live, peers):
    here, width = got[0].shape
    rows = w_query.shape[1] // HEAD_DIM * here
    vmem = pl.BlockSpec(memory_space=pltpu.VMEM)
    return pl.pallas_call(
        functools.partial(keys_kernel, len(got)),
        out_shape=(
            jax.ShapeDtypeStruct((here, width), F32),
            jax.ShapeDtypeStruct((rows, HEAD_DIM), BF16),
            jax.ShapeDtypeStruct((rows, 2 * HEAD_DIM), BF16),
            jax.ShapeDtypeStruct((peers, rows, 2 * HEAD_DIM), BF16),
        ),
        in_specs=[vmem] * (len(got) + 4) + [pl.BlockSpec(memory_space=pltpu.SMEM)],
        out_specs=(vmem,) * 4,
        scratch_shapes=[pltpu.VMEM((rows, width), F32)],
        compiler_params=pltpu.CompilerParams(vmem_limit_bytes=24 * 1024 * 1024),
        name="make_keys",
    )(*got, gain[None, :], w_query, w_key, w_value, live)


def attend(got, query, own, w_out, here):
    rows, width = query.shape[0], w_out.shape[1]
    vmem = pl.BlockSpec(memory_space=pltpu.VMEM)
    return pl.pallas_call(
        attend_kernel,
        out_shape=jax.ShapeDtypeStruct((here, width), F32),
        in_specs=[vmem] * 4,
        out_specs=vmem,
        scratch_shapes=[pltpu.VMEM((rows, width), F32)],
        compiler_params=pltpu.CompilerParams(vmem_limit_bytes=24 * 1024 * 1024),
        name="attend",
    )(got, query, own, w_out)


def shards(
    hidden, span_lengths, section_of, section_live, w_in, norm_gain, w_query, w_key, w_value, w_out
):
    peers = lax.axis_size("seq")
    sections_here = section_live.shape[0]
    sections = sections_here * peers
    swap = [(i, i ^ 1) for i in range(peers)]
    rows, place, level = pool(hidden, span_lengths, section_of, 2, SLOTS, peers, sections)

    def few(_):
        return regroup(rows[0], place[0])

    def some(_):
        return regroup(jnp.concatenate(rows, axis=1), jnp.concatenate(place, axis=1))

    def many(_):
        all_rows, all_place, _ = pool(
            hidden, span_lengths, section_of, 1, sections, peers, sections
        )
        return regroup(all_rows[0], all_place[0])

    pooled = lax.switch(level[0, 0], (few, some, many), 0)
    chips = [[i for i in range(peers) if i % 2 == core] for core in range(2)]
    own, give = project(pooled, w_in, w_query)
    projected = merge(own, lax.ppermute(give, "seq", swap), peers // 2)
    projected = lax.all_to_all(projected, "seq", 0, 0, axis_index_groups=chips, tiled=True)
    doc_in = add_peers(projected, w_key)
    section_in, query, own, sent = make_keys(
        from_segments(doc_in), norm_gain, w_query, w_key, w_value, section_live, peers
    )
    got = lax.all_to_all(sent, "seq", 0, 0, tiled=True)
    terms = attend(got, query, own, w_out, sections_here)
    combined = sum(from_segments(terms))
    return (section_in + combined).astype(BF16)


def solution(mesh):
    in_specs = (
        P("segment", "seq", None),
        P(),
        P(),
        P("seq"),
        P("seq", None),
        P(),
        P(None, "segment"),
        P(None, "segment"),
        P(None, "segment"),
        P("segment", None),
    )
    return jax.shard_map(
        shards, mesh=mesh, in_specs=in_specs, out_specs=P("seq", None), check_vma=False
    )
```

```python
import functools

import jax
import jax.numpy as jnp
from jax import lax
from jax.experimental import pallas as pl
from jax.experimental.pallas import tpu as pltpu
from jax.sharding import PartitionSpec as P

HEAD_DIM = 128
SLOTS = (16, 8)
DEAD = 2.0**100
F32 = jnp.float32
BF16 = jnp.bfloat16
I32 = jnp.int32


def iota(shape, dim):
    return lax.broadcasted_iota(I32, shape, dim)


def below(shape, dim, other):
    return (iota(shape, dim) < iota(shape, other)).astype(F32).astype(BF16)


def turn(row):
    count = row.shape[1]
    same = iota((count, count), 0) == iota((count, count), 1)
    return jnp.sum(jnp.where(same, row, 0), axis=1, keepdims=True)


def turn_back(col):
    count = col.shape[0]
    same = iota((count, count), 0) == iota((count, count), 1)
    return jnp.sum(jnp.where(same, col, 0), axis=0, keepdims=True)


def bits(mask):
    return mask.astype(F32).astype(BF16)


def across(left, right):
    return lax.dot_general(left, right, (((1,), (1,)), ((), ())), preferred_element_type=F32)


def section_at(place, sections, peers):
    half, here = sections // 2, sections // peers
    core = (place >= half).astype(I32)
    left = place - core * half
    chip = left >> (here.bit_length() - 1)
    return left + (chip + core) * here


def pool_kernel(slots, peers, chunks, hidden, lens, secs, *refs):
    groups, every = len(slots), sum(slots)
    offsets = [sum(slots[:g]) for g in range(groups)]
    rows, places, (level, buf, sems) = refs[:groups], refs[groups : 2 * groups], refs[2 * groups :]
    docs, spans = lens.shape
    sections = places[0].shape[-1]
    toks, width = buf.shape
    step = width // chunks
    copies = [
        pltpu.make_async_copy(
            hidden.at[0, :, pl.ds(j * step, step)], buf.at[:, pl.ds(j * step, step)], sems.at[j]
        )
        for j in range(chunks)
    ]
    for copy in copies:
        copy.start()
    doc = lax.axis_index("segment")
    here = lax.axis_index("seq")
    tok0 = (here * toks).astype(F32)
    lengths = lens[...]
    high = (lengths >> 4).astype(F32).astype(BF16)
    low = (lengths & 15).astype(F32).astype(BF16)
    upto = (iota((spans, spans), 0) <= iota((spans, spans), 1)).astype(F32).astype(BF16)
    ends = 16.0 * jnp.dot(high, upto, preferred_element_type=F32)
    ends = ends + jnp.dot(low, upto, preferred_element_type=F32)
    starts = ends - lengths.astype(F32)

    def pick(values):
        own = iota((docs, spans), 0) == doc
        return jnp.sum(jnp.where(own, values, 0), axis=0, keepdims=True)

    end_row = pick(ends)
    start_row = pick(starts)
    sec_row = pick(secs[...])
    section = section_at(iota((sections, 1), 0), sections, peers)
    hits = [section == secs[d : d + 1, :] for d in range(docs)]
    count = sum(hit.astype(F32) for hit in hits)
    count = jnp.sum(count, axis=1, keepdims=True)
    own = section == sec_row
    cover = (start_row < tok0 + toks) & (end_row > tok0)
    present = jnp.max((own & cover).astype(F32), axis=1, keepdims=True)
    ahead = iota((sections, sections), 1) < iota((sections, sections), 0)
    rank = jnp.sum(jnp.where(ahead, turn_back(present), 0.0), axis=1, keepdims=True)
    count_row = jnp.sum(jnp.where(own, count, 0.0), axis=0, keepdims=True)
    slot_row = jnp.sum(jnp.where(own, rank, 0.0), axis=0, keepdims=True)
    weight = 1.0 / jnp.maximum((end_row - start_row) * count_row, 1.0)
    chosen = jnp.where(slot_row == iota((every, spans), 0).astype(F32), weight, 0.0)
    coarse = chosen.astype(BF16).astype(F32)
    split = jnp.concatenate([coarse, chosen - coarse], axis=0).astype(BF16)
    at = tok0 + iota((1, toks), 1).astype(F32)
    inside = (turn(start_row) <= at) & (turn(end_row) > at)
    inside = inside.astype(F32).astype(BF16)
    picked = jnp.dot(split, inside, preferred_element_type=F32)
    picked = picked.astype(BF16)

    peer_width = width // peers

    def work(j):
        copies[j].wait()
        part = jnp.dot(picked, buf[:, j * step : (j + 1) * step], preferred_element_type=F32)
        part = (part[:every] + part[every:]).astype(BF16)
        for i in range(step // peer_width):
            block = part[:, i * peer_width : (i + 1) * peer_width]
            for g in range(groups):
                rows[g][j * (step // peer_width) + i] = block[offsets[g] : offsets[g] + slots[g]]

    for j in range(chunks // 2):
        work(j)

    edge = (iota((peers, 1), 0) * toks).astype(F32)
    before = below((sections, sections), 0, 1)

    def seen(start, end, hit):
        cover = ((start < edge + toks) & (end > edge)).astype(F32).astype(BF16)
        hit = hit.astype(F32).astype(BF16)
        found = lax.dot_general(cover, hit, (((1,), (1,)), ((), ())), preferred_element_type=F32)
        return (found > 0.0).astype(F32)

    mine = seen(start_row, end_row, own)
    order = jnp.dot(mine.astype(BF16), before, preferred_element_type=F32)
    order = jnp.where(mine > 0.0, order, -1.0)
    for q in range(peers):
        for g in range(groups):
            spot = (iota((slots[g], sections), 0) + offsets[g]).astype(F32)
            places[g][q] = (order[q : q + 1, :] == spot).astype(F32).astype(BF16)
    worst = jnp.zeros((peers, 1), F32)
    for d in range(docs):
        held = seen(starts[d : d + 1, :], ends[d : d + 1, :], hits[d])
        worst = jnp.maximum(worst, jnp.sum(held, axis=1, keepdims=True))
    worst = jnp.max(worst, axis=0, keepdims=True)
    tier = (worst > slots[0]).astype(I32) + (worst > every).astype(I32)
    level[...] = jnp.broadcast_to(tier, level.shape)

    for j in range(chunks // 2, chunks):
        work(j)


def pool(hidden, span_lengths, section_of, slots, peers, sections):
    groups = len(slots)
    toks, width = hidden.shape[1:]
    chunks = 8
    vmem = pl.BlockSpec(memory_space=pltpu.VMEM)
    out = pl.pallas_call(
        functools.partial(pool_kernel, slots, peers, chunks),
        out_shape=(
            *[jax.ShapeDtypeStruct((peers, n, width // peers), BF16) for n in slots],
            *[jax.ShapeDtypeStruct((peers, n, sections), BF16) for n in slots],
            jax.ShapeDtypeStruct((1, 128), I32),
        ),
        in_specs=[pl.BlockSpec(memory_space=pl.ANY), vmem, vmem],
        out_specs=(*[vmem] * (2 * groups), vmem),
        scratch_shapes=[pltpu.VMEM((toks, width), BF16), pltpu.SemaphoreType.DMA((chunks,))],
        compiler_params=pltpu.CompilerParams(vmem_limit_bytes=48 * 1024 * 1024),
        name="pool",
    )(hidden, span_lengths, section_of)
    return out[:groups], out[groups : 2 * groups], out[-1]


def regroup(rows, place):
    got = lax.all_to_all(rows, "seq", 0, 0, tiled=True)
    got = got.reshape(-1, got.shape[-1])
    place = place.reshape(-1, place.shape[-1])
    pooled = lax.dot_general(place, got, (((0,), (0,)), ((), ())), preferred_element_type=F32)
    return pooled.astype(BF16)


def from_segments(block):
    size = lax.axis_size("segment")
    others = [
        lax.ppermute(block, "segment", [(i, (i + k) % size) for i in range(size)])
        for k in range(1, size)
    ]
    return [block, *others]


def project_kernel(pooled, w_in, _, own, give):
    half = own.shape[0]
    core = lax.rem(lax.axis_index("seq"), 2)

    def rows(which):
        block = pooled[pl.ds(pl.multiple_of(which * half, half), half), :]
        return jnp.dot(block, w_in[...], preferred_element_type=F32)

    give[...] = rows(1 - core).astype(BF16)
    own[...] = rows(core)


def project(pooled, w_in, ahead):
    half, width = pooled.shape[0] // 2, w_in.shape[1]
    vmem = pl.BlockSpec(memory_space=pltpu.VMEM)
    return pl.pallas_call(
        project_kernel,
        out_shape=(
            jax.ShapeDtypeStruct((half, width), F32),
            jax.ShapeDtypeStruct((half, width), BF16),
        ),
        in_specs=[vmem] * 3,
        out_specs=(vmem, vmem),
        compiler_params=pltpu.CompilerParams(vmem_limit_bytes=24 * 1024 * 1024),
        name="project",
    )(pooled, w_in, ahead)


def merge_kernel(own, pair, out, wide):
    here = out.shape[1]
    wide[...] = own[...] + pair[...].astype(F32)
    for q in range(out.shape[0]):
        out[q] = wide[q * here : (q + 1) * here, :].astype(BF16)


def merge(own, pair, chips):
    half, width = own.shape
    vmem = pl.BlockSpec(memory_space=pltpu.VMEM)
    return pl.pallas_call(
        merge_kernel,
        out_shape=jax.ShapeDtypeStruct((chips, half // chips, width), BF16),
        in_specs=[vmem] * 2,
        out_specs=vmem,
        scratch_shapes=[pltpu.VMEM((half, width), F32)],
        compiler_params=pltpu.CompilerParams(vmem_limit_bytes=24 * 1024 * 1024),
        name="merge",
    )(own, pair)


def add_kernel(got, _, out):
    total = got[0].astype(F32)
    for q in range(1, got.shape[0]):
        total = total + got[q].astype(F32)
    out[...] = total


def add_peers(got, ahead):
    vmem = pl.BlockSpec(memory_space=pltpu.VMEM)
    return pl.pallas_call(
        add_kernel,
        out_shape=jax.ShapeDtypeStruct(got.shape[1:], F32),
        in_specs=[vmem] * 2,
        out_specs=vmem,
        compiler_params=pltpu.CompilerParams(vmem_limit_bytes=24 * 1024 * 1024),
        name="add_peers",
    )(got, ahead)


def by_head(full, here):
    row = iota((full.shape[0], 1), 0) // here
    heads = full.shape[0] // here
    return sum(
        jnp.where(row == h, full[:, h * HEAD_DIM : (h + 1) * HEAD_DIM], 0.0) for h in range(heads)
    )


def keys_kernel(docs, *refs):
    got, refs = refs[:docs], refs[docs:]
    gain, w_query, w_key, w_value, live, section_in, query, own, sent, wide = refs
    here = got[0].shape[0]
    heads = w_query.shape[1] // HEAD_DIM
    total = got[0][...]
    for part in got[1:]:
        total = total + part[...]
    section_in[...] = total
    scale = lax.rsqrt(jnp.mean(total * total, axis=1, keepdims=True) + 1e-05)
    normed = total * scale * gain[...]
    for h in range(heads):
        wide[h * here : (h + 1) * here, :] = normed
    normed = wide[...].astype(BF16)

    def project(weight):
        full = jnp.dot(normed, weight[...], preferred_element_type=F32)
        return by_head(full, here)

    key = project(w_key)
    value = project(w_value)
    spot = lax.rem(iota((heads * here, 1), 0), here)
    alive = jnp.zeros((heads * here, 1), I32)
    for i in range(here):
        alive = jnp.where(spot == i, live[i], alive)
    alive = alive > 0
    flag = jnp.where(iota(key.shape, 1) == 0, F32(DEAD), 0.0)
    pair = jnp.concatenate([jnp.where(alive, key, flag), jnp.where(alive, value, 0.0)], axis=1)
    pair = pair.astype(BF16)
    for q in range(sent.shape[0]):
        sent[q] = pair
    own[...] = jnp.concatenate([key, value], axis=1).astype(BF16)
    query[...] = project(w_query).astype(BF16)


def attend_kernel(got, query, own, w_out, terms, wide):
    peers, rows, _ = got.shape
    here = terms.shape[0]
    heads = rows // here
    both = got[...].reshape(peers * rows, 2 * HEAD_DIM)
    keys, values = both[:, :HEAD_DIM], both[:, HEAD_DIM:]
    q = query[...]
    root = jnp.sqrt(F32(HEAD_DIM))
    scores = across(q, keys) / root
    first = (iota(q.shape, 1) == 0).astype(F32).astype(BF16)
    mark = across(first, keys)
    mine_key = own[:, :HEAD_DIM].astype(F32)
    mine_value = own[:, HEAD_DIM:].astype(F32)
    score = jnp.sum(q.astype(F32) * mine_key, axis=1, keepdims=True) / root
    lane = iota((1, peers * rows), 1)
    row = iota((rows, 1), 0)
    mine = lane == row + lax.axis_index("seq") * rows
    same = lax.rem(lane, rows) // here == row // here
    scores = jnp.where(mark > DEAD * 0.5, F32(-1e30), scores)
    scores = jnp.where(mine, score, scores)
    peak = jnp.max(jnp.where(same, scores, F32(-3e38)), axis=1, keepdims=True)
    probs = jnp.where(same, jnp.exp(scores - peak), 0.0)
    probs = (probs / jnp.sum(probs, axis=1, keepdims=True)).astype(BF16).astype(F32)
    alone = jnp.sum(jnp.where(mine, probs, 0.0), axis=1, keepdims=True)
    rest = jnp.where(mine, 0.0, probs).astype(BF16)
    attended = jnp.dot(rest, values, preferred_element_type=F32) + alone * mine_value
    spread_out = jnp.concatenate([attended] * heads, axis=1)
    block = iota((1, heads * HEAD_DIM), 1) // HEAD_DIM
    spread_out = jnp.where(block == row // here, spread_out, 0.0).astype(BF16)
    wide[...] = jnp.dot(spread_out, w_out[...], preferred_element_type=F32)
    term = wide[0:here, :]
    for h in range(1, heads):
        term = term + wide[h * here : (h + 1) * here, :]
    terms[...] = term


def make_keys(got, gain, w_query, w_key, w_value, live, peers):
    here, width = got[0].shape
    rows = w_query.shape[1] // HEAD_DIM * here
    vmem = pl.BlockSpec(memory_space=pltpu.VMEM)
    return pl.pallas_call(
        functools.partial(keys_kernel, len(got)),
        out_shape=(
            jax.ShapeDtypeStruct((here, width), F32),
            jax.ShapeDtypeStruct((rows, HEAD_DIM), BF16),
            jax.ShapeDtypeStruct((rows, 2 * HEAD_DIM), BF16),
            jax.ShapeDtypeStruct((peers, rows, 2 * HEAD_DIM), BF16),
        ),
        in_specs=[vmem] * (len(got) + 4) + [pl.BlockSpec(memory_space=pltpu.SMEM)],
        out_specs=(vmem,) * 4,
        scratch_shapes=[pltpu.VMEM((rows, width), F32)],
        compiler_params=pltpu.CompilerParams(vmem_limit_bytes=24 * 1024 * 1024),
        name="make_keys",
    )(*got, gain[None, :], w_query, w_key, w_value, live)


def attend(got, query, own, w_out, here):
    rows, width = query.shape[0], w_out.shape[1]
    vmem = pl.BlockSpec(memory_space=pltpu.VMEM)
    return pl.pallas_call(
        attend_kernel,
        out_shape=jax.ShapeDtypeStruct((here, width), F32),
        in_specs=[vmem] * 4,
        out_specs=vmem,
        scratch_shapes=[pltpu.VMEM((rows, width), F32)],
        compiler_params=pltpu.CompilerParams(vmem_limit_bytes=24 * 1024 * 1024),
        name="attend",
    )(got, query, own, w_out)


def shards(
    hidden, span_lengths, section_of, section_live, w_in, norm_gain, w_query, w_key, w_value, w_out
):
    peers = lax.axis_size("seq")
    sections_here = section_live.shape[0]
    sections = sections_here * peers
    swap = [(i, i ^ 1) for i in range(peers)]
    rows, place, level = pool(hidden, span_lengths, section_of, SLOTS, peers, sections)

    def few(_):
        return regroup(rows[0], place[0])

    def some(_):
        return regroup(jnp.concatenate(rows, axis=1), jnp.concatenate(place, axis=1))

    def many(_):
        all_rows, all_place, _ = pool(
            hidden, span_lengths, section_of, (sections,), peers, sections
        )
        return regroup(all_rows[0], all_place[0])

    pooled = lax.switch(level[0, 0], (few, some, many), 0)
    chips = [[i for i in range(peers) if i % 2 == core] for core in range(2)]
    own, give = project(pooled, w_in, w_query)
    projected = merge(own, lax.ppermute(give, "seq", swap), peers // 2)
    projected = lax.all_to_all(projected, "seq", 0, 0, axis_index_groups=chips, tiled=True)
    doc_in = add_peers(projected, w_key)
    section_in, query, own, sent = make_keys(
        from_segments(doc_in), norm_gain, w_query, w_key, w_value, section_live, peers
    )
    got = lax.all_to_all(sent, "seq", 0, 0, tiled=True)
    terms = attend(got, query, own, w_out, sections_here)
    combined = sum(from_segments(terms))
    return (section_in + combined).astype(BF16)


def solution(mesh):
    in_specs = (
        P("segment", "seq", None),
        P(),
        P(),
        P("seq"),
        P("seq", None),
        P(),
        P(None, "segment"),
        P(None, "segment"),
        P(None, "segment"),
        P("segment", None),
    )
    return jax.shard_map(
        shards, mesh=mesh, in_specs=in_specs, out_specs=P("seq", None), check_vma=False
    )
```
